128 devices in a mesh: sweep: 4 (over y), row: 4 (over z), col: 8 (over x, core).
Axes of the slice: x: 4, y: 4, z: 4, core: 2. Of those that a mesh axis runs over, the one named last changes fastest.
Arguments:
- forcing: float32 [8, 2, 8, 32, 4096], P('sweep', None, None, 'row', 'col'), may hold values from -6 to 6
- inverses: bfloat16 [8, 2, 4096, 4096], P('sweep', None, 'col', 'row'), may hold values from -0.0625 to 0.0625
- stiffness: float32 [8, 4096], P('sweep'), may hold values from 0.5 to 2
- pml_layers: int32 [2], replicated, may hold values from 13 to 32
Outputs:
- solution: float32 [8, 2, 8, 32, 4096], P('sweep', None, None, 'row', 'col')
- residual: float32 [4, 2, 8, 32, 4096], P('sweep', None, None, 'row', 'col')
The draws below stay inside these ranges and needn't reach their ends.
Inputs may be any that keep to these rules, and one draw needn't show every extreme that they name: pml_layers[0] counts damping planes at the top, pml_layers[1] at the bottom.
All inputs are finite; a program needn't handle non-finite values.
Results may differ from the reference program's by a relative error of at most 0.018.
Values may be sent and summed in bfloat16 or wider, within the bound.
A program may use at most 64 MiB of HBM per device.

```python
import math
import jax
import jax.numpy as jnp

GX = 64
GY = 64
FRONT = 4096
PANEL_PLANES = 8
PANELS = 8
SRC_ROWS = 32
SRC_COLS = 8


def block_scale(rng, extent, shards, least, top_value):
    def one(axis_at, parts):
        steps = jax.random.uniform(jax.random.fold_in(jax.random.fold_in(rng, 6), axis_at), (parts,), jnp.float32, least / len(shards), top_value / len(shards))
        return jnp.repeat(jnp.exp(steps), extent[axis_at] // parts).reshape((-1,) + (1,) * (len(extent) - axis_at - 1))

    gain = one(*shards[0])
    for cut in shards[1:]:
        gain = gain * one(*cut)
    return gain


def gaussian(key, extent, width, limit, split=(), dtype=jnp.bfloat16):
    drawn = width * jax.random.normal(key, extent, jnp.float32)
    if split:
        drawn = drawn * block_scale(key, extent, split, -0.22, 0.18)
    return jnp.clip(drawn, -limit, limit).astype(dtype)


def setup_inputs(seed: int = 0) -> dict:
    streams_of = jax.random.split(jax.random.key(seed), 5)
    return {
        "forcing": gaussian(streams_of[0], (PANELS, 2, SRC_COLS, SRC_ROWS, FRONT), 1.0, 6.0, ((0, 4), (3, 4), (4, 8)), jnp.float32),
        "inverses": gaussian(streams_of[1], (PANELS, 2, FRONT, FRONT), (2 * FRONT) ** -0.5, 0.0625, ((0, 4), (2, 8), (3, 4))),
        "stiffness": jnp.clip(jnp.exp(math.log(2.0) - 1.3862944 * jax.random.uniform(streams_of[2], (PANELS, FRONT), jnp.float32) ** block_scale(streams_of[2], (PANELS, FRONT), ((0, 4),), -0.2, 0.2)), 0.5, 2.0),
        "pml_layers": jax.random.randint(streams_of[3], (2,), 3 * PANEL_PLANES // 2 + 1, PANEL_PLANES * PANELS // 2 + 1).astype(jnp.int32),
    }


sigma_peak = 2.0


def damping(layers, panel_index, panels_total):
    top_layers = layers[0].astype(jnp.float32)
    bottom_layers = layers[1].astype(jnp.float32)
    centre_plane = jnp.asarray(panel_index).astype(jnp.float32) * PANEL_PLANES + PANEL_PLANES / 2.0
    from_end = panels_total * PANEL_PLANES - centre_plane
    upper = jnp.maximum(top_layers - centre_plane, 0.0) / top_layers
    lower = jnp.maximum(bottom_layers - from_end, 0.0) / bottom_layers
    return sigma_peak * (upper * upper + lower * lower)


def complex_product(load_half, weights):
    in_shape = load_half.shape
    flat_real = load_half[0].reshape(-1, in_shape[-1])
    flat_imag = load_half[1].reshape(-1, in_shape[-1])
    real_part = jnp.dot(flat_real, weights[0], preferred_element_type=jnp.float32) - jnp.dot(flat_imag, weights[1], preferred_element_type=jnp.float32)
    imag_part = jnp.dot(flat_real, weights[1], preferred_element_type=jnp.float32) + jnp.dot(flat_imag, weights[0], preferred_element_type=jnp.float32)
    return jnp.stack([real_part, imag_part]).reshape(2, in_shape[1], in_shape[2], weights.shape[-1])


def plane_apply(wave_field, stiff, sigma):
    lead = wave_field.shape[:-1]
    plane_grid = wave_field.reshape(lead + (GX, GY))
    padded = jnp.pad(plane_grid, ((0, 0), (0, 0), (0, 0), (1, 1), (1, 1)))
    beside = padded[..., 2:, 1:-1] + padded[..., :-2, 1:-1] + padded[..., 1:-1, 2:] + padded[..., 1:-1, :-2]
    beside = beside.reshape(wave_field.shape)
    centre = 6.0 - stiff
    absorb = stiff * sigma
    real_part = centre * wave_field[0] + absorb * wave_field[1] - beside[0]
    imag_part = centre * wave_field[1] - absorb * wave_field[0] - beside[1]
    return jnp.stack([real_part, imag_part])


def reference(forcing, inverses, stiffness, pml_layers):
    previous = jnp.zeros(forcing.shape[1:], jnp.float32)
    solutions = []
    panel_loads = []
    for panel_index in range(PANELS):
        panel_load = forcing[panel_index] + previous
        panel_loads.append(panel_load)
        previous = complex_product(panel_load.astype(jnp.bfloat16), inverses[panel_index])
        solutions.append(previous)
    residuals = []
    for half_index in range(PANELS // 2):
        even_panel = 2 * half_index
        sigma = damping(pml_layers, even_panel, PANELS)
        applied = plane_apply(solutions[even_panel], stiffness[even_panel], sigma)
        residuals.append(panel_loads[even_panel] - applied + solutions[even_panel + 1])
    return jnp.stack(solutions), jnp.stack(residuals)
```

```python
import functools

import jax
import jax.numpy as jnp
from jax import lax
from jax.experimental import pallas as pl
from jax.experimental.pallas import tpu as pltpu
from jax.sharding import PartitionSpec as P

GY = 64
PANEL_PLANES = 8
SIGMA_PEAK = 2.0
MESH = pl.DeviceIdType.MESH
F32 = jnp.float32
BF16 = jnp.bfloat16
ROWS = 16


def sweep_kernel(
    groups, nrow, ncol,
    forcing, inverses, stiffness, pml, solved, residual,
    weights, loads, parts, sib, total, arrive, onward, next_forcing, edge_out, edge_in,
    w_sem, load_recv, load_send, sib_recv, sib_send, arr_recv, arr_send, fwd_send,
    nf_sem, edge_send, edge_recv,
):
    chunks = forcing.shape[2]
    width = forcing.shape[4]
    chips = ncol // 2
    g, r, c = lax.axis_index("sweep"), lax.axis_index("row"), lax.axis_index("col")
    chip, core = c // 2, lax.rem(c, 2)
    sibling = 2 * chip + 1 - core
    home_chip = r == chip
    first, last = g == 0, g == groups - 1
    left_end, right_end = c == 0, c == ncol - 1

    def column(other_row):
        return (g, other_row, c)

    def target(other_row):
        return (g, other_row, 2 * r + core)

    w_copies = [
        pltpu.make_async_copy(inverses.at[p], weights.at[p], w_sem.at[p]) for p in range(2)
    ]
    for copy in w_copies:
        copy.start()

    barrier = pltpu.get_barrier_semaphore()

    def greet(device):
        pl.semaphore_signal(barrier, inc=1, device_id=device, device_id_type=MESH)

    for step in range(1, nrow):
        greet(column(lax.rem(r + step, nrow)))
    greet((g, r, sibling))
    for other in range(nrow):
        @pl.when(jnp.logical_not(jnp.logical_and(home_chip, other == r)))
        def _():
            greet(target(other))
    for other in range(chips):
        @pl.when(jnp.logical_not(jnp.logical_and(home_chip, other == chip)))
        def _():
            greet((g, chip, 2 * other + core))
    for other in range(nrow):
        @pl.when(jnp.logical_not(last))
        def _():
            greet((g + 1, other, c))

        @pl.when(jnp.logical_not(first))
        def _():
            greet((g - 1, other, c))

    @pl.when(jnp.logical_not(left_end))
    def _():
        greet((g, r, c - 1))

    @pl.when(jnp.logical_not(right_end))
    def _():
        greet((g, r, c + 1))

    @pl.when(first)
    def _():
        for k in range(chunks):
            loads[0, k, r] = forcing[0, :, k].reshape(ROWS, width).astype(BF16)

    @pl.when(left_end)
    def _():
        edge_in[0] = jnp.zeros_like(edge_in[0])

    @pl.when(right_end)
    def _():
        edge_in[1] = jnp.zeros_like(edge_in[1])

    expected = (nrow - 1) + 1 + nrow + chips
    expected = expected - 2 * home_chip.astype(jnp.int32)
    expected = expected + nrow * (2 - first.astype(jnp.int32) - last.astype(jnp.int32))
    expected = expected + 2 - left_end.astype(jnp.int32) - right_end.astype(jnp.int32)
    pl.semaphore_wait(barrier, expected)

    def load_copy(p, k, step):
        return pltpu.make_async_remote_copy(
            src_ref=loads.at[p, k, r], dst_ref=loads.at[p, k, r],
            send_sem=load_send.at[p, k, step - 1], recv_sem=load_recv.at[p, k],
            device_id=column(lax.rem(r + step, nrow)), device_id_type=MESH,
        )

    def forward_copy(k, other):
        return pltpu.make_async_remote_copy(
            src_ref=onward.at[k], dst_ref=loads.at[0, k, r],
            send_sem=fwd_send.at[k, other], recv_sem=load_recv.at[0, k],
            device_id=(g + 1, other, c), device_id_type=MESH,
        )

    def sib_copy(p, k):
        return pltpu.make_async_remote_copy(
            src_ref=parts.at[p, k, 1 - core], dst_ref=sib.at[p, k],
            send_sem=sib_send.at[p, k], recv_sem=sib_recv.at[p, k],
            device_id=(g, r, sibling), device_id_type=MESH,
        )

    def home_copy(p, k, other):
        return pltpu.make_async_remote_copy(
            src_ref=total.at[p, k, other], dst_ref=arrive.at[p, k, chip],
            send_sem=arr_send.at[p, k, other], recv_sem=arr_recv.at[p, k],
            device_id=target(other), device_id_type=MESH,
        )

    def nf_copy():
        return pltpu.make_async_remote_copy(
            src_ref=forcing.at[0], dst_ref=next_forcing,
            send_sem=nf_sem.at[0], recv_sem=nf_sem.at[1],
            device_id=(g - 1, r, c), device_id_type=MESH,
        )

    def edge_copy(side):
        return pltpu.make_async_remote_copy(
            src_ref=edge_out.at[side], dst_ref=edge_in.at[1 - side],
            send_sem=edge_send.at[side], recv_sem=edge_recv.at[1 - side],
            device_id=(g, r, c - 1 + 2 * side), device_id_type=MESH,
        )

    def landed(buffer, count, sem):
        some = buffer.at[pl.ds(0, count)]
        pltpu.make_async_copy(some, some, sem).wait()

    def wait_loads(p, k):
        if p == 1:
            landed(loads.at[p, k], nrow - 1, load_recv.at[p, k])
        else:
            @pl.when(first)
            def _():
                landed(loads.at[p, k], nrow - 1, load_recv.at[p, k])

            @pl.when(jnp.logical_not(first))
            def _():
                landed(loads.at[p, k], nrow, load_recv.at[p, k])

    def multiply(p, k):
        wait_loads(p, k)
        rows = nrow * ROWS
        left = loads[p, k].reshape(rows, width)
        by_real = jnp.dot(left, weights[p, 0], preferred_element_type=F32)
        by_imag = jnp.dot(left, weights[p, 1], preferred_element_type=F32)
        by_real = by_real.reshape(nrow, 2, 8, 2 * width)
        by_imag = by_imag.reshape(nrow, 2, 8, 2 * width)
        real = by_real[:, 0] - by_imag[:, 1]
        imag = by_real[:, 1] + by_imag[:, 0]
        both = jnp.concatenate([real[:, None], imag[:, None]], axis=1).reshape(nrow, ROWS, 2 * width)
        both = both.astype(BF16)
        parts[p, k, 0] = both[:, :, :width]
        parts[p, k, 1] = both[:, :, width:]
        sib_copy(p, k).start()

    def combine(p, k):
        sib_copy(p, k).wait_recv()
        whole = parts[p, k, core].astype(F32) + sib[p, k].astype(F32)
        total[p, k] = whole.astype(BF16)

        @pl.when(home_chip)
        def _():
            arrive[p, k, chip] = total[p, k, r]

        for other in range(nrow):
            @pl.when(jnp.logical_not(jnp.logical_and(home_chip, other == r)))
            def _():
                home_copy(p, k, other).start()

    def gather_sum(p, k):
        @pl.when(home_chip)
        def _():
            landed(arrive.at[p, k], chips - 1, arr_recv.at[p, k])

        @pl.when(jnp.logical_not(home_chip))
        def _():
            landed(arrive.at[p, k], chips, arr_recv.at[p, k])

        value = jnp.sum(arrive[p, k].astype(F32), axis=0)
        solved[p, 0, k] = value[:8]
        solved[p, 1, k] = value[8:]
        return value

    def finish_even(k):
        value = gather_sum(0, k)
        source = forcing[1, :, k].reshape(ROWS, width)
        loads[1, k, r] = (value + source).astype(BF16)
        for step in range(1, nrow):
            load_copy(1, k, step).start()
        edge_out[0, k] = value[:, :128].astype(BF16)
        edge_out[1, k] = value[:, width - 128 :].astype(BF16)

    def finish_odd(k):
        value = gather_sum(1, k)

        @pl.when(jnp.logical_not(last))
        def _():
            source = next_forcing[:, k].reshape(ROWS, width)
            onward[k] = (value + source).astype(BF16)
            for other in range(nrow):
                forward_copy(k, other).start()

    @pl.when(first)
    def _():
        for k in range(chunks):
            for step in range(1, nrow):
                load_copy(0, k, step).start()

    @pl.when(jnp.logical_not(first))
    def _():
        nf_copy().start()

    for copy in w_copies:
        copy.wait()

    @pl.when(jnp.logical_not(last))
    def _():
        nf_copy().wait_recv()

    def at(turn, lag, task):
        k = turn - lag

        @pl.when(jnp.logical_and(k >= 0, k < chunks))
        def _():
            task(k)

    def one_turn(turn, carry):
        at(turn, 0, lambda k: multiply(0, k))
        at(turn, 4, finish_odd)
        at(turn, 0, lambda k: combine(0, k))
        at(turn, 2, lambda k: multiply(1, k))
        at(turn, 1, finish_even)

        @pl.when(turn == chunks)
        def _():
            @pl.when(jnp.logical_not(left_end))
            def _():
                edge_copy(0).start()

            @pl.when(jnp.logical_not(right_end))
            def _():
                edge_copy(1).start()

        at(turn, 2, lambda k: combine(1, k))
        return carry

    lax.fori_loop(0, chunks + 4, one_turn, 0)

    @pl.when(jnp.logical_not(left_end))
    def _():
        edge_copy(0).wait_send()

    @pl.when(jnp.logical_not(right_end))
    def _():
        edge_copy(1).wait_send()

    @pl.when(jnp.logical_not(left_end))
    def _():
        edge_copy(1).wait_recv()

    @pl.when(jnp.logical_not(right_end))
    def _():
        edge_copy(0).wait_recv()

    def spread(number):
        return jnp.full((8, width), number, jnp.int32).astype(F32)

    top, bottom = spread(pml[0]), spread(pml[1])
    centre_plane = spread(2 * g).astype(F32) * PANEL_PLANES + PANEL_PLANES / 2.0
    from_end = 2 * groups * PANEL_PLANES - centre_plane
    upper = jnp.maximum(top - centre_plane, 0.0) / top
    lower = jnp.maximum(bottom - from_end, 0.0) / bottom
    sigma = SIGMA_PEAK * (upper * upper + lower * lower)
    begin = pl.multiple_of(c * width, 128)
    stiff = jnp.broadcast_to(stiffness[0:1, pl.ds(begin, width)], (8, width))
    centre = 6.0 - stiff
    absorb = stiff * sigma
    line = lax.rem(lax.broadcasted_iota(jnp.int32, (ROWS, width), 1), GY)
    not_low, not_high = line > 0, line < GY - 1

    def one_residual(k, carry):
        real, imag = solved[0, 0, k], solved[0, 1, k]
        wave = jnp.concatenate([real, imag], axis=0)
        padded = jnp.concatenate(
            [edge_in[0, k].astype(F32), wave, edge_in[1, k].astype(F32)], axis=1
        )
        span = width + 256

        def moved(distance):
            turned = pltpu.roll(padded, distance % span, 1)
            return turned[:, 128 : 128 + width]

        beside = moved(GY) + moved(-GY)
        beside = beside + jnp.where(not_low, moved(1), 0.0) + jnp.where(not_high, moved(-1), 0.0)
        load = loads[0, k, r].astype(F32)
        real_applied = centre * real + absorb * imag - beside[:8]
        imag_applied = centre * imag - absorb * real - beside[8:]
        residual[0, 0, k] = load[:8] - real_applied + solved[1, 0, k]
        residual[0, 1, k] = load[8:] - imag_applied + solved[1, 1, k]
        return carry

    lax.fori_loop(0, chunks, one_residual, 0)

    def drain(k, carry):
        for p in range(2):
            sib_copy(p, k).wait_send()
            for other in range(nrow):
                @pl.when(jnp.logical_not(jnp.logical_and(home_chip, other == r)))
                def _():
                    home_copy(p, k, other).wait_send()
        for step in range(1, nrow):
            load_copy(1, k, step).wait_send()

        @pl.when(first)
        def _():
            for step in range(1, nrow):
                load_copy(0, k, step).wait_send()

        @pl.when(jnp.logical_not(last))
        def _():
            for other in range(nrow):
                forward_copy(k, other).wait_send()

        return carry

    lax.fori_loop(0, chunks, drain, 0)

    @pl.when(jnp.logical_not(first))
    def _():
        nf_copy().wait_send()


def shards(forcing, inverses, stiffness, pml_layers):
    groups, nrow, ncol = (lax.axis_size(name) for name in ("sweep", "row", "col"))
    _, _, chunks, shot_rows, width = forcing.shape
    chips = ncol // 2
    dma = pltpu.SemaphoreType.DMA
    vmem = pl.BlockSpec(memory_space=pltpu.VMEM)
    return pl.pallas_call(
        functools.partial(sweep_kernel, groups, nrow, ncol),
        name="sweep",
        out_shape=(
            jax.ShapeDtypeStruct(forcing.shape, F32),
            jax.ShapeDtypeStruct((1,) + forcing.shape[1:], F32),
        ),
        in_specs=[
            vmem,
            pl.BlockSpec(memory_space=pl.ANY),
            vmem,
            pl.BlockSpec(memory_space=pltpu.SMEM),
        ],
        out_specs=(vmem, vmem),
        scratch_shapes=[
            pltpu.VMEM(inverses.shape, BF16),
            pltpu.VMEM((2, chunks, nrow, ROWS, width), BF16),
            pltpu.VMEM((2, chunks, 2, nrow, ROWS, width), BF16),
            pltpu.VMEM((2, chunks, nrow, ROWS, width), BF16),
            pltpu.VMEM((2, chunks, nrow, ROWS, width), BF16),
            pltpu.VMEM((2, chunks, chips, ROWS, width), BF16),
            pltpu.VMEM((chunks, ROWS, width), BF16),
            pltpu.VMEM(forcing.shape[1:], F32),
            pltpu.VMEM((2, chunks, ROWS, 128), BF16),
            pltpu.VMEM((2, chunks, ROWS, 128), BF16),
            dma((2,)),
            dma((2, chunks)),
            dma((2, chunks, nrow - 1)),
            dma((2, chunks)),
            dma((2, chunks)),
            dma((2, chunks)),
            dma((2, chunks, nrow)),
            dma((chunks, nrow)),
            dma((2,)),
            dma((2,)),
            dma((2,)),
        ],
        compiler_params=pltpu.CompilerParams(
            collective_id=0, has_side_effects=True, vmem_limit_bytes=40 * 1024 * 1024
        ),
        cost_estimate=pl.CostEstimate(
            flops=2 * 2 * 8 * 256 * 512 * 1024, bytes_accessed=6 * 2**20, transcendentals=0
        ),
    )(forcing, inverses, stiffness, pml_layers)


def solution(mesh):
    return jax.shard_map(
        shards,
        mesh=mesh,
        in_specs=(
            P("sweep", None, None, "row", "col"),
            P("sweep", None, "col", "row"),
            P("sweep", None),
            P(),
        ),
        out_specs=(P("sweep", None, None, "row", "col"), P("sweep", None, None, "row", "col")),
        check_vma=False,
    )
```

```python
import functools

import jax
import jax.numpy as jnp
from jax import lax
from jax.experimental import pallas as pl
from jax.experimental.pallas import tpu as pltpu
from jax.sharding import PartitionSpec as P

GY = 64
PANEL_PLANES = 8
SIGMA_PEAK = 2.0
MESH = pl.DeviceIdType.MESH
F32 = jnp.float32
BF16 = jnp.bfloat16
ORDER = (
    ("Ae", 0), ("Co", 7), ("Ao", 4), ("Be", 0), ("Bo", 4), ("Re", 1), ("Ro", 5), ("Ce", 2),
)
ROWS = 16


def sweep_kernel(
    groups, nrow, ncol,
    forcing_hbm, inverses, stiffness, pml, solved, residual,
    weights, sources, loads, parts, sib, total, middle, arrive, onward, next_forcing, edge_out, edge_in,
    stiff_here, w_sem, in_sem, mid_send, mid_recv, load_recv, load_send, sib_recv, sib_send, arr_recv, arr_send, fwd_send,
    nf_sem, edge_send, edge_recv,
):
    chunks = forcing_hbm.shape[2]
    width = forcing_hbm.shape[4]
    forcing = sources
    chips = ncol // 2
    g, r, c = lax.axis_index("sweep"), lax.axis_index("row"), lax.axis_index("col")
    chip, core = c // 2, lax.rem(c, 2)
    sibling = 2 * chip + 1 - core
    first, last = g == 0, g == groups - 1
    left_end, right_end = c == 0, c == ncol - 1

    def column(other_row):
        return (g, other_row, c)

    def along(other_chip):
        return (g, r, 2 * other_chip + core)

    w_copies = [
        pltpu.make_async_copy(inverses.at[p], weights.at[p], w_sem.at[p]) for p in range(2)
    ]
    begin = pl.multiple_of(c * width, 128)
    in_copies = [
        pltpu.make_async_copy(forcing_hbm.at[0], sources.at[0], in_sem.at[0]),
        pltpu.make_async_copy(forcing_hbm.at[1], sources.at[1], in_sem.at[1]),
        pltpu.make_async_copy(stiffness, stiff_here, in_sem.at[2]),
    ]
    for copy in in_copies + w_copies:
        copy.start()

    barrier = pltpu.get_barrier_semaphore()

    def greet(device):
        pl.semaphore_signal(barrier, inc=1, device_id=device, device_id_type=MESH)

    for step in range(1, nrow):
        greet(column(lax.rem(r + step, nrow)))
    greet((g, r, sibling))
    for step in range(1, chips):
        greet(along(lax.rem(chip + step, chips)))
    for other in range(nrow):
        @pl.when(jnp.logical_not(last))
        def _():
            greet((g + 1, other, c))

        @pl.when(jnp.logical_not(first))
        def _():
            greet((g - 1, other, c))

    @pl.when(jnp.logical_not(left_end))
    def _():
        greet((g, r, c - 1))

    @pl.when(jnp.logical_not(right_end))
    def _():
        greet((g, r, c + 1))

    in_copies[0].wait()

    @pl.when(first)
    def _():
        for k in range(chunks):
            loads[0, k, r] = forcing[0, :, k].reshape(ROWS, width).astype(BF16)

    @pl.when(left_end)
    def _():
        edge_in[0] = jnp.zeros_like(edge_in[0])

    @pl.when(right_end)
    def _():
        edge_in[1] = jnp.zeros_like(edge_in[1])

    expected = (nrow - 1) + 1 + (chips - 1)
    expected = expected + nrow * (2 - first.astype(jnp.int32) - last.astype(jnp.int32))
    expected = expected + 2 - left_end.astype(jnp.int32) - right_end.astype(jnp.int32)
    pl.semaphore_wait(barrier, expected)

    def load_copy(p, k, step):
        return pltpu.make_async_remote_copy(
            src_ref=loads.at[p, k, r], dst_ref=loads.at[p, k, r],
            send_sem=load_send.at[p, k, step - 1], recv_sem=load_recv.at[p, k],
            device_id=column(lax.rem(r + step, nrow)), device_id_type=MESH,
        )

    def forward_copy(k, other):
        return pltpu.make_async_remote_copy(
            src_ref=onward.at[k], dst_ref=loads.at[0, k, r],
            send_sem=fwd_send.at[k, other], recv_sem=load_recv.at[0, k],
            device_id=(g + 1, other, c), device_id_type=MESH,
        )

    def sib_copy(p, k):
        return pltpu.make_async_remote_copy(
            src_ref=parts.at[p, k, 1 - core], dst_ref=sib.at[p, k],
            send_sem=sib_send.at[p, k], recv_sem=sib_recv.at[p, k],
            device_id=(g, r, sibling), device_id_type=MESH,
        )

    def middle_copy(p, k, step):
        other = lax.rem(r + step, nrow)
        return pltpu.make_async_remote_copy(
            src_ref=total.at[p, k, other], dst_ref=middle.at[p, k, r],
            send_sem=mid_send.at[p, k, step - 1], recv_sem=mid_recv.at[p, k],
            device_id=column(other), device_id_type=MESH,
        )

    def home_copy(p, k, step):
        other = lax.rem(chip + step, chips)
        return pltpu.make_async_remote_copy(
            src_ref=middle.at[p, k, other], dst_ref=arrive.at[p, k, chip],
            send_sem=arr_send.at[p, k, step - 1], recv_sem=arr_recv.at[p, k],
            device_id=along(other), device_id_type=MESH,
        )

    def nf_copy():
        return pltpu.make_async_remote_copy(
            src_ref=sources.at[0], dst_ref=next_forcing,
            send_sem=nf_sem.at[0], recv_sem=nf_sem.at[1],
            device_id=(g - 1, r, c), device_id_type=MESH,
        )

    def edge_copy(side):
        return pltpu.make_async_remote_copy(
            src_ref=edge_out.at[side], dst_ref=edge_in.at[1 - side],
            send_sem=edge_send.at[side], recv_sem=edge_recv.at[1 - side],
            device_id=(g, r, c - 1 + 2 * side), device_id_type=MESH,
        )

    def landed(buffer, count, sem):
        some = buffer.at[pl.ds(0, count)]
        pltpu.make_async_copy(some, some, sem).wait()

    def wait_loads(p, k):
        if p == 1:
            landed(loads.at[p, k], nrow - 1, load_recv.at[p, k])
        else:
            @pl.when(first)
            def _():
                landed(loads.at[p, k], nrow - 1, load_recv.at[p, k])

            @pl.when(jnp.logical_not(first))
            def _():
                landed(loads.at[p, k], nrow, load_recv.at[p, k])

    def multiply(p, k):
        wait_loads(p, k)
        rows = nrow * ROWS
        left = loads[p, k].reshape(rows, width)
        by_real = jnp.dot(left, weights[p, 0], preferred_element_type=F32)
        by_imag = jnp.dot(left, weights[p, 1], preferred_element_type=F32)
        by_real = by_real.reshape(nrow, 2, 8, 2 * width)
        by_imag = by_imag.reshape(nrow, 2, 8, 2 * width)
        real = by_real[:, 0] - by_imag[:, 1]
        imag = by_real[:, 1] + by_imag[:, 0]
        both = jnp.concatenate([real[:, None], imag[:, None]], axis=1).reshape(nrow, ROWS, 2 * width)
        both = both.astype(BF16)
        parts[p, k, 0] = both[:, :, :width]
        parts[p, k, 1] = both[:, :, width:]
        sib_copy(p, k).start()

    def combine(p, k):
        sib_copy(p, k).wait_recv()
        whole = parts[p, k, core].astype(F32) + sib[p, k].astype(F32)
        total[p, k] = whole.astype(BF16)
        middle[p, k, r] = total[p, k, r]
        for step in range(1, nrow):
            middle_copy(p, k, step).start()

    def pass_on(p, k):
        landed(middle.at[p, k], nrow - 1, mid_recv.at[p, k])
        for step in range(1, chips):
            home_copy(p, k, step).start()
        arrive[p, k, chip] = middle[p, k, chip]

    def gather_sum(p, k):
        landed(arrive.at[p, k], chips - 1, arr_recv.at[p, k])
        value = jnp.sum(arrive[p, k].astype(F32), axis=0)
        solved[p, 0, k] = value[:8]
        solved[p, 1, k] = value[8:]
        return value

    def finish_even(k):
        value = gather_sum(0, k)
        source = forcing[1, :, k].reshape(ROWS, width)
        loads[1, k, r] = (value + source).astype(BF16)
        for step in range(1, nrow):
            load_copy(1, k, step).start()
        edge_out[0, k] = value[:, :128].astype(BF16)
        edge_out[1, k] = value[:, width - 128 :].astype(BF16)

    def finish_odd(k):
        value = gather_sum(1, k)

        @pl.when(jnp.logical_not(last))
        def _():
            source = next_forcing[:, k].reshape(ROWS, width)
            onward[k] = (value + source).astype(BF16)
            for other in range(nrow):
                forward_copy(k, other).start()

    @pl.when(first)
    def _():
        for k in range(chunks):
            for step in range(1, nrow):
                load_copy(0, k, step).start()

    @pl.when(jnp.logical_not(first))
    def _():
        nf_copy().start()

    for copy in in_copies[1:] + w_copies:
        copy.wait()

    @pl.when(jnp.logical_not(last))
    def _():
        nf_copy().wait_recv()

    def at(turn, lag, task):
        k = turn - lag

        @pl.when(jnp.logical_and(k >= 0, k < chunks))
        def _():
            task(k)

    steps = {
        "Ae": lambda k: multiply(0, k),
        "Be": lambda k: combine(0, k),
        "Re": lambda k: pass_on(0, k),
        "Ce": finish_even,
        "Ao": lambda k: multiply(1, k),
        "Bo": lambda k: combine(1, k),
        "Ro": lambda k: pass_on(1, k),
        "Co": finish_odd,
    }

    def one_turn(turn, carry):
        for name, lag in ORDER:
            at(turn, lag, steps[name])
            if name == "Ce":
                @pl.when(turn == chunks - 1 + lag)
                def _():
                    @pl.when(jnp.logical_not(left_end))
                    def _():
                        edge_copy(0).start()

                    @pl.when(jnp.logical_not(right_end))
                    def _():
                        edge_copy(1).start()

        return carry

    lax.fori_loop(0, chunks + max(lag for _, lag in ORDER), one_turn, 0)

    @pl.when(jnp.logical_not(left_end))
    def _():
        edge_copy(0).wait_send()

    @pl.when(jnp.logical_not(right_end))
    def _():
        edge_copy(1).wait_send()

    @pl.when(jnp.logical_not(left_end))
    def _():
        edge_copy(1).wait_recv()

    @pl.when(jnp.logical_not(right_end))
    def _():
        edge_copy(0).wait_recv()

    def spread(number):
        return jnp.full((8, width), number, jnp.int32).astype(F32)

    top, bottom = spread(pml[0]), spread(pml[1])
    centre_plane = spread(2 * g).astype(F32) * PANEL_PLANES + PANEL_PLANES / 2.0
    from_end = 2 * groups * PANEL_PLANES - centre_plane
    upper = jnp.maximum(top - centre_plane, 0.0) / top
    lower = jnp.maximum(bottom - from_end, 0.0) / bottom
    sigma = SIGMA_PEAK * (upper * upper + lower * lower)
    stiff = jnp.broadcast_to(stiff_here[0:1, pl.ds(begin, width)], (8, width))
    centre = 6.0 - stiff
    absorb = stiff * sigma
    line = lax.rem(lax.broadcasted_iota(jnp.int32, (ROWS, width), 1), GY)
    not_low, not_high = line > 0, line < GY - 1

    def one_residual(k, carry):
        real, imag = solved[0, 0, k], solved[0, 1, k]
        wave = jnp.concatenate([real, imag], axis=0)
        padded = jnp.concatenate(
            [edge_in[0, k].astype(F32), wave, edge_in[1, k].astype(F32)], axis=1
        )
        span = width + 256

        def moved(distance):
            turned = pltpu.roll(padded, distance % span, 1)
            return turned[:, 128 : 128 + width]

        beside = moved(GY) + moved(-GY)
        beside = beside + jnp.where(not_low, moved(1), 0.0) + jnp.where(not_high, moved(-1), 0.0)
        load = loads[0, k, r].astype(F32)
        real_applied = centre * real + absorb * imag - beside[:8]
        imag_applied = centre * imag - absorb * real - beside[8:]
        residual[0, 0, k] = load[:8] - real_applied + solved[1, 0, k]
        residual[0, 1, k] = load[8:] - imag_applied + solved[1, 1, k]
        return carry

    lax.fori_loop(0, chunks, one_residual, 0)

    def drain(k, carry):
        for p in range(2):
            sib_copy(p, k).wait_send()
            for step in range(1, nrow):
                middle_copy(p, k, step).wait_send()
            for step in range(1, chips):
                home_copy(p, k, step).wait_send()
        for step in range(1, nrow):
            load_copy(1, k, step).wait_send()

        @pl.when(first)
        def _():
            for step in range(1, nrow):
                load_copy(0, k, step).wait_send()

        @pl.when(jnp.logical_not(last))
        def _():
            for other in range(nrow):
                forward_copy(k, other).wait_send()

        return carry

    lax.fori_loop(0, chunks, drain, 0)

    @pl.when(jnp.logical_not(first))
    def _():
        nf_copy().wait_send()


def shards(forcing, inverses, stiffness, pml_layers):
    groups, nrow, ncol = (lax.axis_size(name) for name in ("sweep", "row", "col"))
    _, _, chunks, shot_rows, width = forcing.shape
    chips = ncol // 2
    dma = pltpu.SemaphoreType.DMA
    vmem = pl.BlockSpec(memory_space=pltpu.VMEM)
    return pl.pallas_call(
        functools.partial(sweep_kernel, groups, nrow, ncol),
        name="sweep",
        out_shape=(
            jax.ShapeDtypeStruct(forcing.shape, F32),
            jax.ShapeDtypeStruct((1,) + forcing.shape[1:], F32),
        ),
        in_specs=[
            pl.BlockSpec(memory_space=pl.ANY),
            pl.BlockSpec(memory_space=pl.ANY),
            pl.BlockSpec(memory_space=pl.ANY),
            pl.BlockSpec(memory_space=pltpu.SMEM),
        ],
        out_specs=(vmem, vmem),
        scratch_shapes=[
            pltpu.VMEM(inverses.shape, BF16),
            pltpu.VMEM(forcing.shape, F32),
            pltpu.VMEM((2, chunks, nrow, ROWS, width), BF16),
            pltpu.VMEM((2, chunks, 2, nrow, ROWS, width), BF16),
            pltpu.VMEM((2, chunks, nrow, ROWS, width), BF16),
            pltpu.VMEM((2, chunks, nrow, ROWS, width), BF16),
            pltpu.VMEM((2, chunks, nrow, ROWS, width), BF16),
            pltpu.VMEM((2, chunks, chips, ROWS, width), BF16),
            pltpu.VMEM((chunks, ROWS, width), BF16),
            pltpu.VMEM(forcing.shape[1:], F32),
            pltpu.VMEM((2, chunks, ROWS, 128), BF16),
            pltpu.VMEM((2, chunks, ROWS, 128), BF16),
            pltpu.VMEM(stiffness.shape, F32),
            dma((2,)),
            dma((3,)),
            dma((2, chunks, nrow - 1)),
            dma((2, chunks)),
            dma((2, chunks)),
            dma((2, chunks, nrow - 1)),
            dma((2, chunks)),
            dma((2, chunks)),
            dma((2, chunks)),
            dma((2, chunks, chips - 1)),
            dma((chunks, nrow)),
            dma((2,)),
            dma((2,)),
            dma((2,)),
        ],
        compiler_params=pltpu.CompilerParams(
            collective_id=0, has_side_effects=True, vmem_limit_bytes=60 * 1024 * 1024
        ),
        cost_estimate=pl.CostEstimate(
            flops=2 * 2 * 8 * 256 * 512 * 1024, bytes_accessed=6 * 2**20, transcendentals=0
        ),
    )(forcing, inverses, stiffness, pml_layers)


def solution(mesh):
    return jax.shard_map(
        shards,
        mesh=mesh,
        in_specs=(
            P("sweep", None, None, "row", "col"),
            P("sweep", None, "col", "row"),
            P("sweep", None),
            P(),
        ),
        out_specs=(P("sweep", None, None, "row", "col"), P("sweep", None, None, "row", "col")),
        check_vma=False,
    )
```

```python
import functools

import jax
import jax.numpy as jnp
from jax import lax
from jax.experimental import pallas as pl
from jax.experimental.pallas import tpu as pltpu
from jax.sharding import PartitionSpec as P

GY = 64
PANEL_PLANES = 8
SIGMA_PEAK = 2.0
MESH = pl.DeviceIdType.MESH
F32 = jnp.float32
BF16 = jnp.bfloat16
PLAIN_ORDER = (
    ("Ce", 3), ("Ae", 0), ("Co", 7), ("Ao", 4), ("Be", 0), ("Re", 1), ("Bo", 4), ("Ro", 5), ("Rs", 29), ("Dr", 36),
)
TURNED_ORDER = (
    ("Ce", 4), ("Co", 5), ("Rs", 5), ("Ao", 3), ("Ae", 0), ("Dr", 5), ("Be", 0), ("Bo", 3), ("Ct", 1),
)
PLAIN_GROUPS = 2
SUB = 1
ROWS = 16


def sweep_kernel(
    groups, nrow, ncol,
    forcing_hbm, inverses, stiffness, pml, solved, residual,
    weights, sources, loads, parts, sib, total, middle, arrive, onward, next_forcing, edge_out, edge_in,
    stiff_here, turned_out, turned_forcing, held, home_out, home_in,
    w_sem, in_sem, turn_sem, out_send, held_recv, pass_send, part_recv,
    home_send, home_recv, mid_send, mid_recv,
    load_recv, load_send, sib_recv, sib_send, arr_recv, arr_send, fwd_send, nf_sem, edge_send, edge_recv,
):
    chunks = forcing_hbm.shape[2]
    width = forcing_hbm.shape[4]
    forcing = sources
    chips = ncol // 2
    g, r, c = lax.axis_index("sweep"), lax.axis_index("row"), lax.axis_index("col")
    chip, core = c // 2, lax.rem(c, 2)
    sibling = 2 * chip + 1 - core
    first, last = g == 0, g == groups - 1
    left_end, right_end = c == 0, c == ncol - 1
    plain = g < PLAIN_GROUPS
    later = jnp.logical_not(plain)
    diagonal = r == chip
    partner = (g, chip, 2 * r + core)
    crossed = jnp.logical_and(later, jnp.logical_not(diagonal))

    def column(other_row):
        return (g, other_row, c)

    def along(other_chip):
        return (g, r, 2 * other_chip + core)

    w_copies = [
        pltpu.make_async_copy(inverses.at[p], weights.at[p], w_sem.at[p]) for p in range(2)
    ]
    begin = pl.multiple_of(c * width, 128)
    in_copies = [
        pltpu.make_async_copy(forcing_hbm.at[0], sources.at[0], in_sem.at[0]),
        pltpu.make_async_copy(forcing_hbm.at[1], sources.at[1], in_sem.at[1]),
        pltpu.make_async_copy(stiffness, stiff_here, in_sem.at[2]),
    ]
    for copy in in_copies + w_copies[:1]:
        copy.start()

    @pl.when(jnp.logical_not(crossed))
    def _():
        w_copies[1].start()

    barrier = pltpu.get_barrier_semaphore()

    def greet(device):
        pl.semaphore_signal(barrier, inc=1, device_id=device, device_id_type=MESH)

    for step in range(1, nrow):
        greet(column(lax.rem(r + step, nrow)))
    greet((g, r, sibling))
    for step in range(1, chips):
        greet(along(lax.rem(chip + step, chips)))
    for other in range(nrow):
        @pl.when(jnp.logical_not(last))
        def _():
            greet((g + 1, other, c))

        @pl.when(jnp.logical_not(first))
        def _():
            greet((g - 1, other, c))

    @pl.when(crossed)
    def _():
        for step in range(1, chips):
            greet((g, chip, 2 * lax.rem(chip + step, chips) + core))
        for step in range(1, nrow):
            greet((g, lax.rem(r + step, nrow), 2 * r + core))

    @pl.when(jnp.logical_not(left_end))
    def _():
        greet((g, r, c - 1))

    @pl.when(jnp.logical_not(right_end))
    def _():
        greet((g, r, c + 1))

    in_copies[0].wait()
    in_copies[1].wait()

    @pl.when(later)
    def _():
        for k in range(chunks):
            turned_out[k] = forcing[1, :, k].reshape(ROWS, width).astype(BF16)

    @pl.when(jnp.logical_and(later, diagonal))
    def _():
        turned_forcing[...] = turned_out[...]

    @pl.when(first)
    def _():
        for k in range(chunks):
            loads[0, k, r] = forcing[0, :, k].reshape(ROWS, width).astype(BF16)

    @pl.when(left_end)
    def _():
        edge_in[0] = jnp.zeros_like(edge_in[0])

    @pl.when(right_end)
    def _():
        edge_in[1] = jnp.zeros_like(edge_in[1])

    expected = (nrow - 1) + 1 + (chips - 1)
    expected = expected + nrow * (2 - first.astype(jnp.int32) - last.astype(jnp.int32))
    expected = expected + (nrow + chips - 2) * crossed.astype(jnp.int32)
    expected = expected + 2 - left_end.astype(jnp.int32) - right_end.astype(jnp.int32)
    pl.semaphore_wait(barrier, expected)

    def load_copy(p, k, step):
        return pltpu.make_async_remote_copy(
            src_ref=loads.at[p, k, r], dst_ref=loads.at[p, k, r],
            send_sem=load_send.at[p, k], recv_sem=load_recv.at[p, k],
            device_id=column(lax.rem(r + step, nrow)), device_id_type=MESH,
        )

    def forward_copy(k, other):
        return pltpu.make_async_remote_copy(
            src_ref=onward.at[k], dst_ref=loads.at[0, k, r],
            send_sem=fwd_send.at[k], recv_sem=load_recv.at[0, k],
            device_id=(g + 1, other, c), device_id_type=MESH,
        )

    def sib_copy(p, k):
        return pltpu.make_async_remote_copy(
            src_ref=parts.at[p, k, 1 - core], dst_ref=sib.at[p, k],
            send_sem=sib_send.at[p, k], recv_sem=sib_recv.at[p, k],
            device_id=(g, r, sibling), device_id_type=MESH,
        )

    def middle_copy(p, k, step):
        other = lax.rem(r + step, nrow)
        return pltpu.make_async_remote_copy(
            src_ref=total.at[p, k, other], dst_ref=middle.at[p, k, r],
            send_sem=mid_send.at[p, k], recv_sem=mid_recv.at[p, k],
            device_id=column(other), device_id_type=MESH,
        )

    def row_copy(p, k, step):
        other = lax.rem(chip + step, chips)
        return pltpu.make_async_remote_copy(
            src_ref=total.at[p, k, other], dst_ref=arrive.at[p, k, chip],
            send_sem=arr_send.at[p, k], recv_sem=arr_recv.at[p, k],
            device_id=along(other), device_id_type=MESH,
        )

    def home_copy(p, k, step):
        other = lax.rem(chip + step, chips)
        return pltpu.make_async_remote_copy(
            src_ref=middle.at[p, k, other], dst_ref=arrive.at[p, k, chip],
            send_sem=arr_send.at[p, k], recv_sem=arr_recv.at[p, k],
            device_id=along(other), device_id_type=MESH,
        )

    def row_load_copy(k, step):
        return pltpu.make_async_remote_copy(
            src_ref=loads.at[1, k, chip], dst_ref=loads.at[1, k, chip],
            send_sem=load_send.at[1, k], recv_sem=load_recv.at[1, k],
            device_id=along(lax.rem(chip + step, chips)), device_id_type=MESH,
        )

    def solved_copy(k):
        return pltpu.make_async_remote_copy(
            src_ref=home_out.at[k], dst_ref=home_in.at[k],
            send_sem=home_send.at[k], recv_sem=home_recv.at[k],
            device_id=partner, device_id_type=MESH,
        )

    part_rows = width // nrow

    def part(index):
        start = index * part_rows
        if not isinstance(index, int):
            start = pl.multiple_of(start, part_rows)
        return pl.ds(start, part_rows)

    def turned_source():
        return pltpu.make_async_remote_copy(
            src_ref=turned_out, dst_ref=turned_forcing,
            send_sem=turn_sem.at[1], recv_sem=turn_sem.at[2],
            device_id=partner, device_id_type=MESH,
        )

    def out_copy(half, q, direct):
        rows = part(q)
        if direct:
            landing, landed_sem = weights.at[1, half, rows], part_recv.at[half, q]
        else:
            landing, landed_sem = held.at[half, r], held_recv.at[half, r]
        return pltpu.make_async_remote_copy(
            src_ref=inverses.at[1, half, rows], dst_ref=landing,
            send_sem=out_send.at[half, q], recv_sem=landed_sem,
            device_id=(g, chip, 2 * q + core) if half == 0 or direct else (g, q, c),
            device_id_type=MESH,
        )

    def held_part(half, source):
        here = held.at[half, source]
        return pltpu.make_async_copy(here, here, held_recv.at[half, source])

    def pass_copy(half, source):
        index = chip if half == 0 else r
        return pltpu.make_async_remote_copy(
            src_ref=held.at[half, source], dst_ref=weights.at[1, half, part(index)],
            send_sem=pass_send.at[half, source], recv_sem=part_recv.at[half, index],
            device_id=(g, r if half == 0 else chip, 2 * source + core), device_id_type=MESH,
        )

    def last_part(half, q):
        here = weights.at[1, half, part(q)]
        return pltpu.make_async_copy(here, here, part_recv.at[half, q])

    def each_out(act):
        for half, step in [(half, step) for half in range(2) for step in range(nrow)]:
                q = lax.rem((chip if half == 0 else r) + step, nrow)

                @pl.when(r == q)
                def _():
                    act(out_copy(half, q, True))

                @pl.when(r != q)
                def _():
                    act(out_copy(half, q, False))

    def each_pass(act):
        for half, step in [(half, step) for half in range(2) for step in range(nrow)]:
                source = lax.rem((r if half == 0 else r) + step, nrow)

                @pl.when(jnp.logical_and(source != r, source != chip))
                def _():
                    act(half, source)

    def nf_copy():
        return pltpu.make_async_remote_copy(
            src_ref=sources.at[0], dst_ref=next_forcing,
            send_sem=nf_sem.at[0], recv_sem=nf_sem.at[1],
            device_id=(g - 1, r, c), device_id_type=MESH,
        )

    def edge_copy(side, k):
        return pltpu.make_async_remote_copy(
            src_ref=edge_out.at[side, k], dst_ref=edge_in.at[1 - side, k],
            send_sem=edge_send.at[side, k], recv_sem=edge_recv.at[1 - side, k],
            device_id=(g, r, c - 1 + 2 * side), device_id_type=MESH,
        )

    def each_edge(act):
        for side, end in ((0, left_end), (1, right_end)):
            @pl.when(jnp.logical_not(end))
            def _():
                act(side)

    def landed(buffer, count, sem):
        some = buffer.at[pl.ds(0, count)]
        pltpu.make_async_copy(some, some, sem).wait()

    def wait_loads(p, k):
        if p == 1:
            landed(loads.at[p, k], nrow - 1, load_recv.at[p, k])

            @pl.when(jnp.logical_and(crossed, k == 0))
            def _():
                for half in range(2):
                    for q in range(nrow):
                        last_part(half, q).wait()
        else:
            @pl.when(first)
            def _():
                landed(loads.at[p, k], nrow - 1, load_recv.at[p, k])

            @pl.when(jnp.logical_not(first))
            def _():
                landed(loads.at[p, k], nrow, load_recv.at[p, k])

    def multiply(p, k):
        wait_loads(p, k)
        rows = nrow * ROWS
        left = loads[p, k].reshape(rows, width)
        by_real = jnp.dot(left, weights[p, 0], preferred_element_type=F32)
        by_imag = jnp.dot(left, weights[p, 1], preferred_element_type=F32)
        by_real = by_real.reshape(nrow, 2, 8, 2 * width)
        by_imag = by_imag.reshape(nrow, 2, 8, 2 * width)
        real = by_real[:, 0] - by_imag[:, 1]
        imag = by_real[:, 1] + by_imag[:, 0]
        both = jnp.concatenate([real[:, None], imag[:, None]], axis=1).reshape(nrow, ROWS, 2 * width)
        both = both.astype(BF16)
        parts[p, k, 0] = both[:, :, :width]
        parts[p, k, 1] = both[:, :, width:]
        sib_copy(p, k).start()

    def combine(p, k):
        sib_copy(p, k).wait_recv()
        whole = parts[p, k, core].astype(F32) + sib[p, k].astype(F32)

        total[p, k] = whole.astype(BF16)

        def to_rows():
            middle[p, k, r] = total[p, k, r]
            for step in range(1, nrow):
                middle_copy(p, k, step).start()

        if p == 1:
            to_rows()
        else:
            pl.when(plain)(to_rows)

            @pl.when(later)
            def _():
                arrive[p, k, chip] = total[p, k, chip]
                for step in range(1, chips):
                    row_copy(p, k, step).start()

    def row_sum(p, k):
        landed(arrive.at[p, k], chips - 1, arr_recv.at[p, k])
        return jnp.sum(arrive[p, k].astype(F32), axis=0)

    def middle_landed(p, k):
        landed(middle.at[p, k], nrow - 1, mid_recv.at[p, k])

    def pass_on(p, k):
        middle_landed(p, k)
        for step in range(1, chips):
            home_copy(p, k, step).start()
        arrive[p, k, chip] = middle[p, k, chip]

    def keep(p, k, value):
        solved[p, 0, k] = value[:8]
        solved[p, 1, k] = value[8:]
        if p == 0:
            edge_out[0, k] = value[:, :128].astype(BF16)
            edge_out[1, k] = value[:, width - 128 :].astype(BF16)
            each_edge(lambda side: edge_copy(side, k).start())

    def forward(k, value):
        keep(1, k, value)

        @pl.when(jnp.logical_not(last))
        def _():
            source = next_forcing[:, k].reshape(ROWS, width)
            onward[k] = (value + source).astype(BF16)
            for other in range(nrow):
                forward_copy(k, other).start()

    def turned_sum(k):
        own = row_sum(0, k)
        loads[1, k, chip] = (own + turned_forcing[k].astype(F32)).astype(BF16)
        for step in range(1, chips):
            row_load_copy(k, step).start()

        @pl.when(diagonal)
        def _():
            keep(0, k, own)

        @pl.when(crossed)
        def _():
            home_out[k] = own.astype(BF16)
            solved_copy(k).start()

    def finish_even(k):
        @pl.when(plain)
        def _():
            value = row_sum(0, k)
            keep(0, k, value)
            source = forcing[1, :, k].reshape(ROWS, width)
            loads[1, k, r] = (value + source).astype(BF16)
            for step in range(1, nrow):
                load_copy(1, k, step).start()

        @pl.when(crossed)
        def _():
            solved_copy(k).wait_recv()
            keep(0, k, home_in[k].astype(F32))

    def finish_odd(k):
        @pl.when(plain)
        def _():
            forward(k, row_sum(1, k))

        @pl.when(later)
        def _():
            middle_landed(1, k)
            forward(k, jnp.sum(middle[1, k].astype(F32), axis=0))

    @pl.when(first)
    def _():
        for k in range(chunks):
            for step in range(1, nrow):
                load_copy(0, k, step).start()

    @pl.when(jnp.logical_not(first))
    def _():
        nf_copy().start()

    @pl.when(crossed)
    def _():
        turned_source().start()
        each_out(lambda copy: copy.start())

    for copy in in_copies[2:] + w_copies[:1]:
        copy.wait()

    @pl.when(jnp.logical_not(crossed))
    def _():
        w_copies[1].wait()

    @pl.when(later)
    def _():
        def pass_part(half, source):
            held_part(half, source).wait()
            pass_copy(half, source).start()

        each_pass(pass_part)

    @pl.when(crossed)
    def _():
        turned_source().wait_recv()

    @pl.when(jnp.logical_not(last))
    def _():
        nf_copy().wait_recv()

    def spread(number):
        return jnp.full((8, width), number, jnp.int32).astype(F32)

    top, bottom = spread(pml[0]), spread(pml[1])
    centre_plane = spread(2 * g).astype(F32) * PANEL_PLANES + PANEL_PLANES / 2.0
    from_end = 2 * groups * PANEL_PLANES - centre_plane
    upper = jnp.maximum(top - centre_plane, 0.0) / top
    lower = jnp.maximum(bottom - from_end, 0.0) / bottom
    sigma = SIGMA_PEAK * (upper * upper + lower * lower)
    stiff = jnp.broadcast_to(stiff_here[0:1, pl.ds(begin, width)], (8, width))
    centre = 6.0 - stiff
    absorb = stiff * sigma
    line = lax.rem(lax.broadcasted_iota(jnp.int32, (ROWS, width), 1), GY)
    not_low, not_high = line > 0, line < GY - 1

    def one_residual(k):
        each_edge(lambda side: edge_copy(1 - side, k).wait_recv())
        real, imag = solved[0, 0, k], solved[0, 1, k]
        wave = jnp.concatenate([real, imag], axis=0)
        padded = jnp.concatenate(
            [edge_in[0, k].astype(F32), wave, edge_in[1, k].astype(F32)], axis=1
        )
        span = width + 256

        def moved(distance):
            turned = pltpu.roll(padded, distance % span, 1)
            return turned[:, 128 : 128 + width]

        beside = moved(GY) + moved(-GY)
        beside = beside + jnp.where(not_low, moved(1), 0.0) + jnp.where(not_high, moved(-1), 0.0)
        load = loads[0, k, r].astype(F32)
        real_applied = centre * real + absorb * imag - beside[:8]
        imag_applied = centre * imag - absorb * real - beside[8:]
        residual[0, 0, k] = load[:8] - real_applied + solved[1, 0, k]
        residual[0, 1, k] = load[8:] - imag_applied + solved[1, 1, k]

    def drain(k):
        for p in range(2):
            sib_copy(p, k).wait_send()
        landed(total.at[1, k], nrow - 1, mid_send.at[1, k])
        landed(loads.at[1, k], nrow - 1, load_send.at[1, k])
        landed(total.at[0, k], chips - 1, arr_send.at[0, k])

        @pl.when(plain)
        def _():
            landed(total.at[0, k], nrow - 1, mid_send.at[0, k])
            landed(middle.at[1, k], chips - 1, arr_send.at[1, k])

        @pl.when(first)
        def _():
            landed(loads.at[0, k], nrow - 1, load_send.at[0, k])

        @pl.when(crossed)
        def _():
            solved_copy(k).wait_send()

        @pl.when(jnp.logical_not(last))
        def _():
            landed(loads.at[0, k], nrow, fwd_send.at[k])

        each_edge(lambda side: edge_copy(side, k).wait_send())

    def at(turn, lag, task):
        k = turn - lag

        @pl.when(jnp.logical_and(k >= 0, k < chunks))
        def _():
            task(k)

    steps = {
        "Ae": lambda k: multiply(0, k),
        "Be": lambda k: combine(0, k),
        "Re": lambda k: pass_on(0, k),
        "Ce": finish_even,
        "Ct": turned_sum,
        "Rs": one_residual,
        "Dr": drain,
        "Ao": lambda k: multiply(1, k),
        "Bo": lambda k: combine(1, k),
        "Ro": lambda k: pass_on(1, k),
        "Co": finish_odd,
    }

    def run(order):
        def one_turn(turn, carry):
            for name, lag in order:
                at(turn, lag, steps[name])
            return carry

        lax.fori_loop(0, chunks + max(lag for _, lag in order), one_turn, 0)

    @pl.when(plain)
    def _():
        run(PLAIN_ORDER)

    @pl.when(later)
    def _():
        run(TURNED_ORDER)

    @pl.when(crossed)
    def _():
        turned_source().wait_send()
        each_out(lambda copy: copy.wait_send())

    @pl.when(later)
    def _():
        each_pass(lambda half, source: pass_copy(half, source).wait_send())

    @pl.when(jnp.logical_not(first))
    def _():
        nf_copy().wait_send()


def shards(forcing, inverses, stiffness, pml_layers):
    groups, nrow, ncol = (lax.axis_size(name) for name in ("sweep", "row", "col"))
    _, _, chunks, shot_rows, width = forcing.shape
    chips = ncol // 2
    dma = pltpu.SemaphoreType.DMA
    vmem = pl.BlockSpec(memory_space=pltpu.VMEM)
    return pl.pallas_call(
        functools.partial(sweep_kernel, groups, nrow, ncol),
        name="sweep",
        out_shape=(
            jax.ShapeDtypeStruct(forcing.shape, F32),
            jax.ShapeDtypeStruct((1,) + forcing.shape[1:], F32),
        ),
        in_specs=[
            pl.BlockSpec(memory_space=pl.ANY),
            pl.BlockSpec(memory_space=pl.ANY),
            pl.BlockSpec(memory_space=pl.ANY),
            pl.BlockSpec(memory_space=pltpu.SMEM),
        ],
        out_specs=(vmem, vmem),
        scratch_shapes=[
            pltpu.VMEM(inverses.shape, BF16),
            pltpu.VMEM(forcing.shape, F32),
            pltpu.VMEM((2, chunks, nrow, ROWS, width), BF16),
            pltpu.VMEM((2, chunks, 2, nrow, ROWS, width), BF16),
            pltpu.VMEM((2, chunks, nrow, ROWS, width), BF16),
            pltpu.VMEM((2, chunks, nrow, ROWS, width), BF16),
            pltpu.VMEM((2, chunks, nrow, ROWS, width), BF16),
            pltpu.VMEM((2, chunks, chips, ROWS, width), BF16),
            pltpu.VMEM((chunks, ROWS, width), BF16),
            pltpu.VMEM(forcing.shape[1:], F32),
            pltpu.VMEM((2, chunks, ROWS, 128), BF16),
            pltpu.VMEM((2, chunks, ROWS, 128), BF16),
            pltpu.VMEM(stiffness.shape, F32),
            pltpu.VMEM((chunks, ROWS, width), BF16),
            pltpu.VMEM((chunks, ROWS, width), BF16),
            pltpu.VMEM((2, nrow, width // nrow, 2 * width), BF16),
            pltpu.VMEM((chunks, ROWS, width), BF16),
            pltpu.VMEM((chunks, ROWS, width), BF16),
            dma((2,)),
            dma((3,)),
            dma((5,)),
            dma((2, nrow)),
            dma((2, nrow)),
            dma((2, nrow)),
            dma((2, nrow)),
            dma((chunks,)),
            dma((chunks,)),
            dma((2, chunks)),
            dma((2, chunks)),
            dma((2, chunks)),
            dma((2, chunks)),
            dma((2, chunks)),
            dma((2, chunks)),
            dma((2, chunks)),
            dma((2, chunks)),
            dma((chunks,)),
            dma((2,)),
            dma((2, chunks)),
            dma((2, chunks)),
        ],
        compiler_params=pltpu.CompilerParams(
            collective_id=0, has_side_effects=True, vmem_limit_bytes=52 * 1024 * 1024
        ),
        cost_estimate=pl.CostEstimate(
            flops=2 * 2 * 8 * 256 * 512 * 1024, bytes_accessed=6 * 2**20, transcendentals=0
        ),
    )(forcing, inverses, stiffness, pml_layers)


def solution(mesh):
    return jax.shard_map(
        shards,
        mesh=mesh,
        in_specs=(
            P("sweep", None, None, "row", "col"),
            P("sweep", None, "col", "row"),
            P("sweep", None),
            P(),
        ),
        out_specs=(P("sweep", None, None, "row", "col"), P("sweep", None, None, "row", "col")),
        check_vma=False,
    )
```

```python
import functools

import jax
import jax.numpy as jnp
from jax import lax
from jax.experimental import pallas as pl
from jax.experimental.pallas import tpu as pltpu
from jax.sharding import PartitionSpec as P

GY = 64
PANEL_PLANES = 8
SIGMA_PEAK = 2.0
MESH = pl.DeviceIdType.MESH
F32 = jnp.float32
BF16 = jnp.bfloat16
FIRST_ORDER = (
    ("Ae", 0), ("Ce", 4), ("Rs", 12), ("Dr", 19), ("Ao", 6), ("Re", 2), ("Co", 10), ("Ro", 8), ("Be", 0), ("Bo", 6),
)
PLAIN_ORDER = (
    ("Dr", 18), ("Ao", 6), ("Co", 9), ("Ce", 4), ("Ae", 0), ("Re", 2), ("Bo", 6), ("Be", 0), ("Rs", 12), ("Ro", 7),
)
TURNED_ORDER = (
    ("Dr", 7), ("Co", 5), ("Ae", 0), ("Ao", 3), ("Rs", 5), ("Be", 0), ("Bo", 3), ("Ce", 3), ("Ct", 1),
)
PLAIN_GROUPS = 2
WAY_STEPS = lambda n: range(n)
WAY_HALVES = (0, 1)
SUB = 2
ROWS = 16


def sweep_kernel(
    groups, nrow, ncol,
    forcing_hbm, inverses, stiffness, pml, solved, residual,
    weights, sources, loads, parts, sib, total, middle, arrive, onward, next_forcing, edge_out, edge_in,
    stiff_here, turned_out, turned_forcing, held, home_out, home_in,
    w_sem, in_sem, turn_sem, out_send, held_recv, pass_send, part_recv,
    home_send, home_recv, mid_send, mid_recv,
    load_recv, load_send, sib_recv, sib_send, arr_recv, arr_send, fwd_send, nf_sem, edge_send, edge_recv,
):
    chunks = forcing_hbm.shape[2]
    width = forcing_hbm.shape[4]
    forcing = sources
    chips = ncol // 2
    g, r, c = lax.axis_index("sweep"), lax.axis_index("row"), lax.axis_index("col")
    chip, core = c // 2, lax.rem(c, 2)
    sibling = 2 * chip + 1 - core
    first, last = g == 0, g == groups - 1
    left_end, right_end = c == 0, c == ncol - 1
    plain = g < PLAIN_GROUPS
    later = jnp.logical_not(plain)
    diagonal = r == chip
    partner = (g, chip, 2 * r + core)
    crossed = jnp.logical_and(later, jnp.logical_not(diagonal))

    def column(other_row):
        return (g, other_row, c)

    def along(other_chip):
        return (g, r, 2 * other_chip + core)

    w_copies = [
        pltpu.make_async_copy(inverses.at[p], weights.at[p], w_sem.at[p]) for p in range(2)
    ]
    begin = pl.multiple_of(c * width, 128)
    in_copies = [
        pltpu.make_async_copy(forcing_hbm.at[0], sources.at[0], in_sem.at[0]),
        pltpu.make_async_copy(forcing_hbm.at[1], sources.at[1], in_sem.at[1]),
        pltpu.make_async_copy(stiffness, stiff_here, in_sem.at[2]),
    ]
    for copy in in_copies + w_copies[:1]:
        copy.start()

    @pl.when(jnp.logical_not(crossed))
    def _():
        w_copies[1].start()

    barrier = pltpu.get_barrier_semaphore()

    def greet(device):
        pl.semaphore_signal(barrier, inc=1, device_id=device, device_id_type=MESH)

    for step in range(1, nrow):
        greet(column(lax.rem(r + step, nrow)))
    greet((g, r, sibling))
    for step in range(1, chips):
        greet(along(lax.rem(chip + step, chips)))
    for other in range(nrow):
        @pl.when(jnp.logical_not(last))
        def _():
            greet((g + 1, other, c))

        @pl.when(jnp.logical_not(first))
        def _():
            greet((g - 1, other, c))

    @pl.when(crossed)
    def _():
        for step in range(1, chips):
            greet((g, chip, 2 * lax.rem(chip + step, chips) + core))
        for step in range(1, nrow):
            greet((g, lax.rem(r + step, nrow), 2 * r + core))

    @pl.when(jnp.logical_not(left_end))
    def _():
        greet((g, r, c - 1))

    @pl.when(jnp.logical_not(right_end))
    def _():
        greet((g, r, c + 1))

    @pl.when(first)
    def _():
        in_copies[0].wait()
        for k in range(chunks):
            loads[0, k, r] = forcing[0, :, k].reshape(ROWS, width).astype(BF16)

    @pl.when(left_end)
    def _():
        edge_in[0] = jnp.zeros_like(edge_in[0])

    @pl.when(right_end)
    def _():
        edge_in[1] = jnp.zeros_like(edge_in[1])

    expected = (nrow - 1) + 1 + (chips - 1)
    expected = expected + nrow * (2 - first.astype(jnp.int32) - last.astype(jnp.int32))
    expected = expected + (nrow + chips - 2) * crossed.astype(jnp.int32)
    expected = expected + 2 - left_end.astype(jnp.int32) - right_end.astype(jnp.int32)
    pl.semaphore_wait(barrier, expected)

    def load_copy(p, k, step):
        return pltpu.make_async_remote_copy(
            src_ref=loads.at[p, k, r], dst_ref=loads.at[p, k, r],
            send_sem=load_send.at[p, k], recv_sem=load_recv.at[p, k],
            device_id=column(lax.rem(r + step, nrow)), device_id_type=MESH,
        )

    def forward_copy(k, other):
        return pltpu.make_async_remote_copy(
            src_ref=onward.at[k], dst_ref=loads.at[0, k, r],
            send_sem=fwd_send.at[k], recv_sem=load_recv.at[0, k],
            device_id=(g + 1, other, c), device_id_type=MESH,
        )

    def sib_copy(p, k):
        return pltpu.make_async_remote_copy(
            src_ref=parts.at[p, k, 1 - core], dst_ref=sib.at[p, k],
            send_sem=sib_send.at[p, k], recv_sem=sib_recv.at[p, k],
            device_id=(g, r, sibling), device_id_type=MESH,
        )

    def middle_copy(p, k, step):
        other = lax.rem(r + step, nrow)
        return pltpu.make_async_remote_copy(
            src_ref=total.at[p, k, other], dst_ref=middle.at[p, k, r],
            send_sem=mid_send.at[p, k], recv_sem=mid_recv.at[p, k],
            device_id=column(other), device_id_type=MESH,
        )

    def row_copy(p, k, step):
        other = lax.rem(chip + step, chips)
        return pltpu.make_async_remote_copy(
            src_ref=total.at[p, k, other], dst_ref=arrive.at[p, k, chip],
            send_sem=arr_send.at[p, k], recv_sem=arr_recv.at[p, k],
            device_id=along(other), device_id_type=MESH,
        )

    def home_copy(p, k, step):
        other = lax.rem(chip + step, chips)
        return pltpu.make_async_remote_copy(
            src_ref=middle.at[p, k, other], dst_ref=arrive.at[p, k, chip],
            send_sem=arr_send.at[p, k], recv_sem=arr_recv.at[p, k],
            device_id=along(other), device_id_type=MESH,
        )

    def row_load_copy(k, step):
        return pltpu.make_async_remote_copy(
            src_ref=loads.at[1, k, chip], dst_ref=loads.at[1, k, chip],
            send_sem=load_send.at[1, k], recv_sem=load_recv.at[1, k],
            device_id=along(lax.rem(chip + step, chips)), device_id_type=MESH,
        )

    def solved_copy(k):
        return pltpu.make_async_remote_copy(
            src_ref=home_out.at[k], dst_ref=home_in.at[k],
            send_sem=home_send.at[k], recv_sem=home_recv.at[k],
            device_id=partner, device_id_type=MESH,
        )

    part_rows = width // nrow

    sub_rows = part_rows // SUB

    def part(index, sub=None):
        start = index * part_rows
        if sub is None:
            return pl.ds(pl.multiple_of(start, part_rows), part_rows)
        return pl.ds(pl.multiple_of(start + sub * sub_rows, sub_rows), sub_rows)

    def turned_source():
        return pltpu.make_async_remote_copy(
            src_ref=turned_out, dst_ref=turned_forcing,
            send_sem=turn_sem.at[1], recv_sem=turn_sem.at[2],
            device_id=partner, device_id_type=MESH,
        )

    def out_copy(half, q, sub, direct):
        rows = part(q, sub)
        if direct:
            landing, landed_sem = weights.at[1, half, rows], part_recv.at[half, q]
        else:
            landing, landed_sem = held.at[half, r, part(0, sub)], held_recv.at[half, r, sub]
        return pltpu.make_async_remote_copy(
            src_ref=inverses.at[1, half, rows], dst_ref=landing,
            send_sem=out_send.at[half, q], recv_sem=landed_sem,
            device_id=(g, chip, 2 * q + core) if half == 0 or direct else (g, q, c),
            device_id_type=MESH,
        )

    def held_part(half, source, sub):
        here = held.at[half, source, part(0, sub)]
        return pltpu.make_async_copy(here, here, held_recv.at[half, source, sub])

    def pass_copy(half, source, sub):
        index = chip if half == 0 else r
        return pltpu.make_async_remote_copy(
            src_ref=held.at[half, source, part(0, sub)],
            dst_ref=weights.at[1, half, part(index, sub)],
            send_sem=pass_send.at[half, source], recv_sem=part_recv.at[half, index],
            device_id=(g, r if half == 0 else chip, 2 * source + core), device_id_type=MESH,
        )

    def whole_part(half, q, sem):
        here = weights.at[1, half, part(q)]
        return pltpu.make_async_copy(here, here, sem)

    ways = [(half, step) for step in WAY_STEPS(nrow) for half in WAY_HALVES]

    def start_out():
        for sub in range(SUB):
            for half, step in ways:
                q = lax.rem((chip if half == 0 else r) + step, nrow)

                @pl.when(r == q)
                def _():
                    out_copy(half, q, sub, True).start()

                @pl.when(r != q)
                def _():
                    out_copy(half, q, sub, False).start()

    def each_pass(act):
        for half, step in ways:
            source = lax.rem(r + step, nrow)

            @pl.when(jnp.logical_and(source != r, source != chip))
            def _():
                act(half, source)

    def nf_copy():
        return pltpu.make_async_remote_copy(
            src_ref=forcing_hbm.at[0], dst_ref=next_forcing,
            send_sem=nf_sem.at[0], recv_sem=nf_sem.at[1],
            device_id=(g - 1, r, c), device_id_type=MESH,
        )

    def edge_copy(side, k):
        return pltpu.make_async_remote_copy(
            src_ref=edge_out.at[side, k], dst_ref=edge_in.at[1 - side, k],
            send_sem=edge_send.at[side, k], recv_sem=edge_recv.at[1 - side, k],
            device_id=(g, r, c - 1 + 2 * side), device_id_type=MESH,
        )

    def each_edge(act):
        for side, end in ((0, left_end), (1, right_end)):
            @pl.when(jnp.logical_not(end))
            def _():
                act(side)

    def landed(buffer, count, sem):
        some = buffer.at[pl.ds(0, count)]
        pltpu.make_async_copy(some, some, sem).wait()

    def wait_loads(p, k):
        if p == 1:
            landed(loads.at[p, k], nrow - 1, load_recv.at[p, k])

            @pl.when(jnp.logical_and(jnp.logical_not(crossed), k == 0))
            def _():
                w_copies[1].wait()

            @pl.when(jnp.logical_and(crossed, k == 0))
            def _():
                for half in range(2):
                    for q in range(nrow):
                        whole_part(half, q, part_recv.at[half, q]).wait()
        else:
            @pl.when(first)
            def _():
                landed(loads.at[p, k], nrow - 1, load_recv.at[p, k])

            @pl.when(jnp.logical_not(first))
            def _():
                landed(loads.at[p, k], nrow, load_recv.at[p, k])

    def multiply(p, k):
        wait_loads(p, k)
        rows = nrow * ROWS
        left = loads[p, k].reshape(rows, width)
        by_real = jnp.dot(left, weights[p, 0], preferred_element_type=F32)
        by_imag = jnp.dot(left, weights[p, 1], preferred_element_type=F32)
        by_real = by_real.reshape(nrow, 2, 8, 2 * width)
        by_imag = by_imag.reshape(nrow, 2, 8, 2 * width)
        real = by_real[:, 0] - by_imag[:, 1]
        imag = by_real[:, 1] + by_imag[:, 0]
        both = jnp.concatenate([real[:, None], imag[:, None]], axis=1).reshape(nrow, ROWS, 2 * width)
        both = both.astype(BF16)
        parts[p, k, 0] = both[:, :, :width]
        parts[p, k, 1] = both[:, :, width:]
        sib_copy(p, k).start()

    def combine(p, k):
        sib_copy(p, k).wait_recv()
        whole = parts[p, k, core].astype(F32) + sib[p, k].astype(F32)

        total[p, k] = whole.astype(BF16)

        def to_rows():
            middle[p, k, r] = total[p, k, r]
            for step in range(1, nrow):
                middle_copy(p, k, step).start()

        if p == 1:
            to_rows()
        else:
            pl.when(plain)(to_rows)

            @pl.when(later)
            def _():
                arrive[p, k, chip] = total[p, k, chip]
                for step in range(1, chips):
                    row_copy(p, k, step).start()

    def row_sum(p, k):
        landed(arrive.at[p, k], chips - 1, arr_recv.at[p, k])
        return jnp.sum(arrive[p, k].astype(F32), axis=0)

    def middle_landed(p, k):
        landed(middle.at[p, k], nrow - 1, mid_recv.at[p, k])

    def pass_on(p, k):
        middle_landed(p, k)
        for step in range(1, chips):
            home_copy(p, k, step).start()
        arrive[p, k, chip] = middle[p, k, chip]

    def keep(p, k, value):
        solved[p, 0, k] = value[:8]
        solved[p, 1, k] = value[8:]
        if p == 0:
            edge_out[0, k] = value[:, :128].astype(BF16)
            edge_out[1, k] = value[:, width - 128 :].astype(BF16)
            each_edge(lambda side: edge_copy(side, k).start())

    def forward(k, value):
        keep(1, k, value)

        @pl.when(jnp.logical_and(jnp.logical_not(last), k == 0))
        def _():
            nf_copy().wait_recv()

        @pl.when(jnp.logical_not(last))
        def _():
            source = next_forcing[:, k].reshape(ROWS, width)
            onward[k] = (value + source).astype(BF16)
            for other in range(nrow):
                forward_copy(k, other).start()

    def turned_sum(k):
        own = row_sum(0, k)
        loads[1, k, chip] = (own + turned_forcing[k].astype(F32)).astype(BF16)
        for step in range(1, chips):
            row_load_copy(k, step).start()

        @pl.when(diagonal)
        def _():
            keep(0, k, own)

        @pl.when(crossed)
        def _():
            home_out[k] = own.astype(BF16)
            solved_copy(k).start()

    def finish_even(k):
        @pl.when(plain)
        def _():
            value = row_sum(0, k)
            keep(0, k, value)
            source = forcing[1, :, k].reshape(ROWS, width)
            loads[1, k, r] = (value + source).astype(BF16)
            for step in range(1, nrow):
                load_copy(1, k, step).start()

        @pl.when(crossed)
        def _():
            solved_copy(k).wait_recv()
            keep(0, k, home_in[k].astype(F32))

    def finish_odd(k):
        @pl.when(plain)
        def _():
            forward(k, row_sum(1, k))

        @pl.when(later)
        def _():
            middle_landed(1, k)
            forward(k, jnp.sum(middle[1, k].astype(F32), axis=0))

    @pl.when(first)
    def _():
        for k in range(chunks):
            for step in range(1, nrow):
                load_copy(0, k, step).start()

    @pl.when(jnp.logical_not(first))
    def _():
        nf_copy().start()

    pl.when(crossed)(start_out)

    @pl.when(later)
    def _():
        in_copies[1].wait()
        for k in range(chunks):
            turned_out[k] = forcing[1, :, k].reshape(ROWS, width).astype(BF16)

        @pl.when(diagonal)
        def _():
            turned_forcing[...] = turned_out[...]

        @pl.when(crossed)
        def _():
            turned_source().start()

    w_copies[0].wait()

    @pl.when(later)
    def _():
        for sub in range(SUB):
            def pass_part(half, source):
                held_part(half, source, sub).wait()
                pass_copy(half, source, sub).start()

            each_pass(pass_part)

    @pl.when(crossed)
    def _():
        turned_source().wait_recv()

    @pl.when(plain)
    def _():
        in_copies[1].wait()

    @pl.when(jnp.logical_not(first))
    def _():
        in_copies[0].wait()

    in_copies[2].wait()

    def spread(number):
        return jnp.full((8, width), number, jnp.int32).astype(F32)

    top, bottom = spread(pml[0]), spread(pml[1])
    centre_plane = spread(2 * g).astype(F32) * PANEL_PLANES + PANEL_PLANES / 2.0
    from_end = 2 * groups * PANEL_PLANES - centre_plane
    upper = jnp.maximum(top - centre_plane, 0.0) / top
    lower = jnp.maximum(bottom - from_end, 0.0) / bottom
    sigma = SIGMA_PEAK * (upper * upper + lower * lower)
    stiff = jnp.broadcast_to(stiff_here[0:1, pl.ds(begin, width)], (8, width))
    centre = 6.0 - stiff
    absorb = stiff * sigma
    line = lax.rem(lax.broadcasted_iota(jnp.int32, (ROWS, width), 1), GY)
    not_low, not_high = line > 0, line < GY - 1

    def one_residual(k):
        each_edge(lambda side: edge_copy(1 - side, k).wait_recv())
        real, imag = solved[0, 0, k], solved[0, 1, k]
        wave = jnp.concatenate([real, imag], axis=0)
        padded = jnp.concatenate(
            [edge_in[0, k].astype(F32), wave, edge_in[1, k].astype(F32)], axis=1
        )
        span = width + 256

        def moved(distance):
            turned = pltpu.roll(padded, distance % span, 1)
            return turned[:, 128 : 128 + width]

        beside = moved(GY) + moved(-GY)
        beside = beside + jnp.where(not_low, moved(1), 0.0) + jnp.where(not_high, moved(-1), 0.0)
        load = loads[0, k, r].astype(F32)
        real_applied = centre * real + absorb * imag - beside[:8]
        imag_applied = centre * imag - absorb * real - beside[8:]
        residual[0, 0, k] = load[:8] - real_applied + solved[1, 0, k]
        residual[0, 1, k] = load[8:] - imag_applied + solved[1, 1, k]

    def drain(k):
        for p in range(2):
            sib_copy(p, k).wait_send()
        landed(total.at[1, k], nrow - 1, mid_send.at[1, k])
        landed(loads.at[1, k], nrow - 1, load_send.at[1, k])
        landed(total.at[0, k], chips - 1, arr_send.at[0, k])

        @pl.when(plain)
        def _():
            landed(total.at[0, k], nrow - 1, mid_send.at[0, k])
            landed(middle.at[1, k], chips - 1, arr_send.at[1, k])

        @pl.when(first)
        def _():
            landed(loads.at[0, k], nrow - 1, load_send.at[0, k])

        @pl.when(crossed)
        def _():
            solved_copy(k).wait_send()

        @pl.when(jnp.logical_not(last))
        def _():
            landed(loads.at[0, k], nrow, fwd_send.at[k])

        each_edge(lambda side: edge_copy(side, k).wait_send())

    def at(turn, lag, task):
        k = turn - lag

        @pl.when(jnp.logical_and(k >= 0, k < chunks))
        def _():
            task(k)

    steps = {
        "Ae": lambda k: multiply(0, k),
        "Be": lambda k: combine(0, k),
        "Re": lambda k: pass_on(0, k),
        "Ce": finish_even,
        "Ct": turned_sum,
        "Rs": one_residual,
        "Dr": drain,
        "Ao": lambda k: multiply(1, k),
        "Bo": lambda k: combine(1, k),
        "Ro": lambda k: pass_on(1, k),
        "Co": finish_odd,
    }

    def run(order):
        def one_turn(turn, carry):
            for name, lag in order:
                at(turn, lag, steps[name])
            return carry

        lax.fori_loop(0, chunks + max(lag for _, lag in order), one_turn, 0)

    @pl.when(first)
    def _():
        run(FIRST_ORDER)

    @pl.when(jnp.logical_and(plain, jnp.logical_not(first)))
    def _():
        run(PLAIN_ORDER)

    @pl.when(later)
    def _():
        run(TURNED_ORDER)

    @pl.when(crossed)
    def _():
        turned_source().wait_send()
        for half in range(2):
            for q in range(nrow):
                whole_part(half, q, out_send.at[half, q]).wait()

    @pl.when(later)
    def _():
        each_pass(lambda half, source: whole_part(half, 0, pass_send.at[half, source]).wait())

    @pl.when(jnp.logical_not(first))
    def _():
        nf_copy().wait_send()


def shards(forcing, inverses, stiffness, pml_layers):
    groups, nrow, ncol = (lax.axis_size(name) for name in ("sweep", "row", "col"))
    _, _, chunks, shot_rows, width = forcing.shape
    chips = ncol // 2
    dma = pltpu.SemaphoreType.DMA
    vmem = pl.BlockSpec(memory_space=pltpu.VMEM)
    return pl.pallas_call(
        functools.partial(sweep_kernel, groups, nrow, ncol),
        name="sweep",
        out_shape=(
            jax.ShapeDtypeStruct(forcing.shape, F32),
            jax.ShapeDtypeStruct((1,) + forcing.shape[1:], F32),
        ),
        in_specs=[
            pl.BlockSpec(memory_space=pl.ANY),
            pl.BlockSpec(memory_space=pl.ANY),
            pl.BlockSpec(memory_space=pl.ANY),
            pl.BlockSpec(memory_space=pltpu.SMEM),
        ],
        out_specs=(vmem, vmem),
        scratch_shapes=[
            pltpu.VMEM(inverses.shape, BF16),
            pltpu.VMEM(forcing.shape, F32),
            pltpu.VMEM((2, chunks, nrow, ROWS, width), BF16),
            pltpu.VMEM((2, chunks, 2, nrow, ROWS, width), BF16),
            pltpu.VMEM((2, chunks, nrow, ROWS, width), BF16),
            pltpu.VMEM((2, chunks, nrow, ROWS, width), BF16),
            pltpu.VMEM((2, chunks, nrow, ROWS, width), BF16),
            pltpu.VMEM((2, chunks, chips, ROWS, width), BF16),
            pltpu.VMEM((chunks, ROWS, width), BF16),
            pltpu.VMEM(forcing.shape[1:], F32),
            pltpu.VMEM((2, chunks, ROWS, 128), BF16),
            pltpu.VMEM((2, chunks, ROWS, 128), BF16),
            pltpu.VMEM(stiffness.shape, F32),
            pltpu.VMEM((chunks, ROWS, width), BF16),
            pltpu.VMEM((chunks, ROWS, width), BF16),
            pltpu.VMEM((2, nrow, width // nrow, 2 * width), BF16),
            pltpu.VMEM((chunks, ROWS, width), BF16),
            pltpu.VMEM((chunks, ROWS, width), BF16),
            dma((2,)),
            dma((3,)),
            dma((5,)),
            dma((2, nrow)),
            dma((2, nrow, SUB)),
            dma((2, nrow)),
            dma((2, nrow)),
            dma((chunks,)),
            dma((chunks,)),
            dma((2, chunks)),
            dma((2, chunks)),
            dma((2, chunks)),
            dma((2, chunks)),
            dma((2, chunks)),
            dma((2, chunks)),
            dma((2, chunks)),
            dma((2, chunks)),
            dma((chunks,)),
            dma((2,)),
            dma((2, chunks)),
            dma((2, chunks)),
        ],
        compiler_params=pltpu.CompilerParams(
            collective_id=0, has_side_effects=True, vmem_limit_bytes=53 * 1024 * 1024
        ),
        cost_estimate=pl.CostEstimate(
            flops=2 * 2 * 8 * 256 * 512 * 1024, bytes_accessed=6 * 2**20, transcendentals=0
        ),
    )(forcing, inverses, stiffness, pml_layers)


def solution(mesh):
    return jax.shard_map(
        shards,
        mesh=mesh,
        in_specs=(
            P("sweep", None, None, "row", "col"),
            P("sweep", None, "col", "row"),
            P("sweep", None),
            P(),
        ),
        out_specs=(P("sweep", None, None, "row", "col"), P("sweep", None, None, "row", "col")),
        check_vma=False,
    )
```

```python
import functools

import jax
import jax.numpy as jnp
from jax import lax
from jax.experimental import pallas as pl
from jax.experimental.pallas import tpu as pltpu
from jax.sharding import PartitionSpec as P

GY = 64
PANEL_PLANES = 8
SIGMA_PEAK = 2.0
MESH = pl.DeviceIdType.MESH
F32 = jnp.float32
BF16 = jnp.bfloat16
FIRST_ORDER = (
    ("Ae", 0), ("Ce", 4), ("Rs", 12), ("Dr", 19), ("Ao", 6), ("Re", 2), ("Co", 10), ("Ro", 8), ("Be", 0), ("Bo", 6),
)
PLAIN_ORDER = (
    ("Dr", 18), ("Ao", 6), ("Co", 9), ("Ce", 4), ("Ae", 0), ("Re", 2), ("Bo", 6), ("Be", 0), ("Rs", 12), ("Ro", 7),
)
TURNED_ORDER = (
    ("Dr", 7), ("Co", 5), ("Ae", 0), ("Ao", 3), ("Rs", 5), ("Be", 0), ("Bo", 3), ("Ce", 3), ("Ct", 1),
)
PLAIN_GROUPS = 2
WAY_STEPS = lambda n: range(n)
WAY_HALVES = (0, 1)
SUB = 2
ROWS = 16


def far_first(count):
    return sorted(range(1, count), key=lambda step: -min(step, count - step))


def sweep_kernel(
    groups, nrow, ncol,
    forcing_hbm, inverses, stiffness, pml, solved, residual,
    weights, sources, loads, parts, sib, total, middle, arrive, onward, next_forcing, edge_out, edge_in,
    stiff_here, turned_out, turned_forcing, held, home_out, home_in,
    w_sem, in_sem, turn_sem, out_send, held_recv, pass_send, part_recv,
    home_send, home_recv, mid_send, mid_recv,
    load_recv, load_send, sib_recv, sib_send, arr_recv, arr_send, fwd_send, nf_sem, edge_send, edge_recv,
):
    chunks = forcing_hbm.shape[2]
    width = forcing_hbm.shape[4]
    forcing = sources
    chips = ncol // 2
    g, r, c = lax.axis_index("sweep"), lax.axis_index("row"), lax.axis_index("col")
    chip, core = c // 2, lax.rem(c, 2)
    sibling = 2 * chip + 1 - core
    first, last = g == 0, g == groups - 1
    left_end, right_end = c == 0, c == ncol - 1
    plain = g < PLAIN_GROUPS
    later = jnp.logical_not(plain)
    diagonal = r == chip
    partner = (g, chip, 2 * r + core)
    crossed = jnp.logical_and(later, jnp.logical_not(diagonal))

    def column(other_row):
        return (g, other_row, c)

    def along(other_chip):
        return (g, r, 2 * other_chip + core)

    w_copies = [
        pltpu.make_async_copy(inverses.at[p], weights.at[p], w_sem.at[p]) for p in range(2)
    ]
    begin = pl.multiple_of(c * width, 128)
    in_copies = [
        pltpu.make_async_copy(forcing_hbm.at[0], sources.at[0], in_sem.at[0]),
        pltpu.make_async_copy(forcing_hbm.at[1], sources.at[1], in_sem.at[1]),
        pltpu.make_async_copy(stiffness, stiff_here, in_sem.at[2]),
    ]
    for copy in in_copies + w_copies[:1]:
        copy.start()

    @pl.when(jnp.logical_not(crossed))
    def _():
        w_copies[1].start()

    barrier = pltpu.get_barrier_semaphore()

    def greet(device):
        pl.semaphore_signal(barrier, inc=1, device_id=device, device_id_type=MESH)

    for step in far_first(nrow):
        greet(column(lax.rem(r + step, nrow)))
    greet((g, r, sibling))
    for step in far_first(chips):
        greet(along(lax.rem(chip + step, chips)))
    for other in range(nrow):
        @pl.when(jnp.logical_not(last))
        def _():
            greet((g + 1, other, c))

        @pl.when(jnp.logical_not(first))
        def _():
            greet((g - 1, other, c))

    @pl.when(crossed)
    def _():
        for step in far_first(chips):
            greet((g, chip, 2 * lax.rem(chip + step, chips) + core))
        for step in far_first(nrow):
            greet((g, lax.rem(r + step, nrow), 2 * r + core))

    @pl.when(jnp.logical_not(left_end))
    def _():
        greet((g, r, c - 1))

    @pl.when(jnp.logical_not(right_end))
    def _():
        greet((g, r, c + 1))

    @pl.when(first)
    def _():
        in_copies[0].wait()
        for k in range(chunks):
            loads[0, k, r] = forcing[0, :, k].reshape(ROWS, width).astype(BF16)

    @pl.when(left_end)
    def _():
        edge_in[0] = jnp.zeros_like(edge_in[0])

    @pl.when(right_end)
    def _():
        edge_in[1] = jnp.zeros_like(edge_in[1])

    expected = (nrow - 1) + 1 + (chips - 1)
    expected = expected + nrow * (2 - first.astype(jnp.int32) - last.astype(jnp.int32))
    expected = expected + (nrow + chips - 2) * crossed.astype(jnp.int32)
    expected = expected + 2 - left_end.astype(jnp.int32) - right_end.astype(jnp.int32)
    pl.semaphore_wait(barrier, expected)

    def load_copy(p, k, step):
        return pltpu.make_async_remote_copy(
            src_ref=loads.at[p, k, r], dst_ref=loads.at[p, k, r],
            send_sem=load_send.at[p, k], recv_sem=load_recv.at[p, k],
            device_id=column(lax.rem(r + step, nrow)), device_id_type=MESH,
        )

    def forward_copy(k, other):
        return pltpu.make_async_remote_copy(
            src_ref=onward.at[k], dst_ref=loads.at[0, k, r],
            send_sem=fwd_send.at[k], recv_sem=load_recv.at[0, k],
            device_id=(g + 1, other, c), device_id_type=MESH,
        )

    def sib_copy(p, k):
        return pltpu.make_async_remote_copy(
            src_ref=parts.at[p, k, 1 - core], dst_ref=sib.at[p, k],
            send_sem=sib_send.at[p, k], recv_sem=sib_recv.at[p, k],
            device_id=(g, r, sibling), device_id_type=MESH,
        )

    def middle_copy(p, k, step):
        other = lax.rem(r + step, nrow)
        return pltpu.make_async_remote_copy(
            src_ref=total.at[p, k, other], dst_ref=middle.at[p, k, r],
            send_sem=mid_send.at[p, k], recv_sem=mid_recv.at[p, k],
            device_id=column(other), device_id_type=MESH,
        )

    def row_copy(p, k, step):
        other = lax.rem(chip + step, chips)
        return pltpu.make_async_remote_copy(
            src_ref=total.at[p, k, other], dst_ref=arrive.at[p, k, chip],
            send_sem=arr_send.at[p, k], recv_sem=arr_recv.at[p, k],
            device_id=along(other), device_id_type=MESH,
        )

    def home_copy(p, k, step):
        other = lax.rem(chip + step, chips)
        return pltpu.make_async_remote_copy(
            src_ref=middle.at[p, k, other], dst_ref=arrive.at[p, k, chip],
            send_sem=arr_send.at[p, k], recv_sem=arr_recv.at[p, k],
            device_id=along(other), device_id_type=MESH,
        )

    def row_load_copy(k, step):
        return pltpu.make_async_remote_copy(
            src_ref=loads.at[1, k, chip], dst_ref=loads.at[1, k, chip],
            send_sem=load_send.at[1, k], recv_sem=load_recv.at[1, k],
            device_id=along(lax.rem(chip + step, chips)), device_id_type=MESH,
        )

    def solved_copy(k):
        return pltpu.make_async_remote_copy(
            src_ref=home_out.at[k], dst_ref=home_in.at[k],
            send_sem=home_send.at[k], recv_sem=home_recv.at[k],
            device_id=partner, device_id_type=MESH,
        )

    part_rows = width // nrow

    sub_rows = part_rows // SUB

    def part(index, sub=None):
        start = index * part_rows
        if sub is None:
            return pl.ds(pl.multiple_of(start, part_rows), part_rows)
        return pl.ds(pl.multiple_of(start + sub * sub_rows, sub_rows), sub_rows)

    def turned_source():
        return pltpu.make_async_remote_copy(
            src_ref=turned_out, dst_ref=turned_forcing,
            send_sem=turn_sem.at[1], recv_sem=turn_sem.at[2],
            device_id=partner, device_id_type=MESH,
        )

    def out_copy(half, q, sub, direct):
        rows = part(q, sub)
        if direct:
            landing, landed_sem = weights.at[1, half, rows], part_recv.at[half, q]
        else:
            landing, landed_sem = held.at[half, r, part(0, sub)], held_recv.at[half, r, sub]
        return pltpu.make_async_remote_copy(
            src_ref=inverses.at[1, half, rows], dst_ref=landing,
            send_sem=out_send.at[half, q], recv_sem=landed_sem,
            device_id=(g, chip, 2 * q + core) if half == 0 or direct else (g, q, c),
            device_id_type=MESH,
        )

    def held_part(half, source, sub):
        here = held.at[half, source, part(0, sub)]
        return pltpu.make_async_copy(here, here, held_recv.at[half, source, sub])

    def pass_copy(half, source, sub):
        index = chip if half == 0 else r
        return pltpu.make_async_remote_copy(
            src_ref=held.at[half, source, part(0, sub)],
            dst_ref=weights.at[1, half, part(index, sub)],
            send_sem=pass_send.at[half, source], recv_sem=part_recv.at[half, index],
            device_id=(g, r if half == 0 else chip, 2 * source + core), device_id_type=MESH,
        )

    def whole_part(half, q, sem):
        here = weights.at[1, half, part(q)]
        return pltpu.make_async_copy(here, here, sem)

    ways = [(half, step) for step in WAY_STEPS(nrow) for half in WAY_HALVES]

    def start_out():
        for sub in range(SUB):
            for half, step in ways:
                q = lax.rem((chip if half == 0 else r) + step, nrow)

                @pl.when(r == q)
                def _():
                    out_copy(half, q, sub, True).start()

                @pl.when(r != q)
                def _():
                    out_copy(half, q, sub, False).start()

    def each_pass(act):
        for half, step in ways:
            source = lax.rem(r + step, nrow)

            @pl.when(jnp.logical_and(source != r, source != chip))
            def _():
                act(half, source)

    def nf_copy():
        return pltpu.make_async_remote_copy(
            src_ref=forcing_hbm.at[0], dst_ref=next_forcing,
            send_sem=nf_sem.at[0], recv_sem=nf_sem.at[1],
            device_id=(g - 1, r, c), device_id_type=MESH,
        )

    def edge_copy(side, k):
        return pltpu.make_async_remote_copy(
            src_ref=edge_out.at[side, k], dst_ref=edge_in.at[1 - side, k],
            send_sem=edge_send.at[side, k], recv_sem=edge_recv.at[1 - side, k],
            device_id=(g, r, c - 1 + 2 * side), device_id_type=MESH,
        )

    def each_edge(act):
        for side, end in ((0, left_end), (1, right_end)):
            @pl.when(jnp.logical_not(end))
            def _():
                act(side)

    def landed(buffer, count, sem):
        some = buffer.at[pl.ds(0, count)]
        pltpu.make_async_copy(some, some, sem).wait()

    def wait_loads(p, k):
        if p == 1:
            landed(loads.at[p, k], nrow - 1, load_recv.at[p, k])

            @pl.when(jnp.logical_and(jnp.logical_not(crossed), k == 0))
            def _():
                w_copies[1].wait()

            @pl.when(jnp.logical_and(crossed, k == 0))
            def _():
                for half in range(2):
                    for q in range(nrow):
                        whole_part(half, q, part_recv.at[half, q]).wait()
        else:
            @pl.when(first)
            def _():
                landed(loads.at[p, k], nrow - 1, load_recv.at[p, k])

            @pl.when(jnp.logical_not(first))
            def _():
                landed(loads.at[p, k], nrow, load_recv.at[p, k])

    def multiply(p, k):
        wait_loads(p, k)
        rows = nrow * ROWS
        left = loads[p, k].reshape(rows, width)
        by_real = jnp.dot(left, weights[p, 0], preferred_element_type=F32)
        by_imag = jnp.dot(left, weights[p, 1], preferred_element_type=F32)
        by_real = by_real.reshape(nrow, 2, 8, 2 * width)
        by_imag = by_imag.reshape(nrow, 2, 8, 2 * width)
        real = by_real[:, 0] - by_imag[:, 1]
        imag = by_real[:, 1] + by_imag[:, 0]
        both = jnp.concatenate([real[:, None], imag[:, None]], axis=1).reshape(nrow, ROWS, 2 * width)
        both = both.astype(BF16)
        parts[p, k, 0] = both[:, :, :width]
        parts[p, k, 1] = both[:, :, width:]
        sib_copy(p, k).start()

    def combine(p, k):
        sib_copy(p, k).wait_recv()
        whole = parts[p, k, core].astype(F32) + sib[p, k].astype(F32)

        total[p, k] = whole.astype(BF16)

        def to_rows():
            middle[p, k, r] = total[p, k, r]
            for step in far_first(nrow):
                middle_copy(p, k, step).start()

        if p == 1:
            to_rows()
        else:
            pl.when(plain)(to_rows)

            @pl.when(later)
            def _():
                arrive[p, k, chip] = total[p, k, chip]
                for step in far_first(chips):
                    row_copy(p, k, step).start()

    def row_sum(p, k):
        landed(arrive.at[p, k], chips - 1, arr_recv.at[p, k])
        return jnp.sum(arrive[p, k].astype(F32), axis=0)

    def middle_landed(p, k):
        landed(middle.at[p, k], nrow - 1, mid_recv.at[p, k])

    def pass_on(p, k):
        middle_landed(p, k)
        for step in far_first(chips):
            home_copy(p, k, step).start()
        arrive[p, k, chip] = middle[p, k, chip]

    def keep(p, k, value):
        solved[p, 0, k] = value[:8]
        solved[p, 1, k] = value[8:]
        if p == 0:
            edge_out[0, k] = value[:, :128].astype(BF16)
            edge_out[1, k] = value[:, width - 128 :].astype(BF16)
            each_edge(lambda side: edge_copy(side, k).start())

    def forward(k, value):
        keep(1, k, value)

        @pl.when(jnp.logical_and(jnp.logical_not(last), k == 0))
        def _():
            nf_copy().wait_recv()

        @pl.when(jnp.logical_not(last))
        def _():
            source = next_forcing[:, k].reshape(ROWS, width)
            onward[k] = (value + source).astype(BF16)
            for step in far_first(nrow) + [0]:
                forward_copy(k, lax.rem(r + step, nrow)).start()

    def turned_sum(k):
        own = row_sum(0, k)
        loads[1, k, chip] = (own + turned_forcing[k].astype(F32)).astype(BF16)
        for step in far_first(chips):
            row_load_copy(k, step).start()

        @pl.when(diagonal)
        def _():
            keep(0, k, own)

        @pl.when(crossed)
        def _():
            home_out[k] = own.astype(BF16)
            solved_copy(k).start()

    def finish_even(k):
        @pl.when(plain)
        def _():
            value = row_sum(0, k)
            keep(0, k, value)
            source = forcing[1, :, k].reshape(ROWS, width)
            loads[1, k, r] = (value + source).astype(BF16)
            for step in far_first(nrow):
                load_copy(1, k, step).start()

        @pl.when(crossed)
        def _():
            solved_copy(k).wait_recv()
            keep(0, k, home_in[k].astype(F32))

    def finish_odd(k):
        @pl.when(plain)
        def _():
            forward(k, row_sum(1, k))

        @pl.when(later)
        def _():
            middle_landed(1, k)
            forward(k, jnp.sum(middle[1, k].astype(F32), axis=0))

    @pl.when(first)
    def _():
        for k in range(chunks):
            for step in far_first(nrow):
                load_copy(0, k, step).start()

    @pl.when(jnp.logical_not(first))
    def _():
        nf_copy().start()

    pl.when(crossed)(start_out)

    @pl.when(later)
    def _():
        in_copies[1].wait()
        for k in range(chunks):
            turned_out[k] = forcing[1, :, k].reshape(ROWS, width).astype(BF16)

        @pl.when(diagonal)
        def _():
            turned_forcing[...] = turned_out[...]

        @pl.when(crossed)
        def _():
            turned_source().start()

    w_copies[0].wait()

    @pl.when(later)
    def _():
        for sub in range(SUB):
            def pass_part(half, source):
                held_part(half, source, sub).wait()
                pass_copy(half, source, sub).start()

            each_pass(pass_part)

    @pl.when(crossed)
    def _():
        turned_source().wait_recv()

    @pl.when(plain)
    def _():
        in_copies[1].wait()

    @pl.when(jnp.logical_not(first))
    def _():
        in_copies[0].wait()

    in_copies[2].wait()

    def spread(number):
        return jnp.full((8, width), number, jnp.int32).astype(F32)

    top, bottom = spread(pml[0]), spread(pml[1])
    centre_plane = spread(2 * g).astype(F32) * PANEL_PLANES + PANEL_PLANES / 2.0
    from_end = 2 * groups * PANEL_PLANES - centre_plane
    upper = jnp.maximum(top - centre_plane, 0.0) / top
    lower = jnp.maximum(bottom - from_end, 0.0) / bottom
    sigma = SIGMA_PEAK * (upper * upper + lower * lower)
    stiff = jnp.broadcast_to(stiff_here[0:1, pl.ds(begin, width)], (8, width))
    centre = 6.0 - stiff
    absorb = stiff * sigma
    line = lax.rem(lax.broadcasted_iota(jnp.int32, (ROWS, width), 1), GY)
    not_low, not_high = line > 0, line < GY - 1

    def one_residual(k):
        each_edge(lambda side: edge_copy(1 - side, k).wait_recv())
        real, imag = solved[0, 0, k], solved[0, 1, k]
        wave = jnp.concatenate([real, imag], axis=0)
        padded = jnp.concatenate(
            [edge_in[0, k].astype(F32), wave, edge_in[1, k].astype(F32)], axis=1
        )
        span = width + 256

        def moved(distance):
            turned = pltpu.roll(padded, distance % span, 1)
            return turned[:, 128 : 128 + width]

        beside = moved(GY) + moved(-GY)
        beside = beside + jnp.where(not_low, moved(1), 0.0) + jnp.where(not_high, moved(-1), 0.0)
        load = loads[0, k, r].astype(F32)
        real_applied = centre * real + absorb * imag - beside[:8]
        imag_applied = centre * imag - absorb * real - beside[8:]
        residual[0, 0, k] = load[:8] - real_applied + solved[1, 0, k]
        residual[0, 1, k] = load[8:] - imag_applied + solved[1, 1, k]

    def drain(k):
        for p in range(2):
            sib_copy(p, k).wait_send()
        landed(total.at[1, k], nrow - 1, mid_send.at[1, k])
        landed(loads.at[1, k], nrow - 1, load_send.at[1, k])
        landed(total.at[0, k], chips - 1, arr_send.at[0, k])

        @pl.when(plain)
        def _():
            landed(total.at[0, k], nrow - 1, mid_send.at[0, k])
            landed(middle.at[1, k], chips - 1, arr_send.at[1, k])

        @pl.when(first)
        def _():
            landed(loads.at[0, k], nrow - 1, load_send.at[0, k])

        @pl.when(crossed)
        def _():
            solved_copy(k).wait_send()

        @pl.when(jnp.logical_not(last))
        def _():
            landed(loads.at[0, k], nrow, fwd_send.at[k])

        each_edge(lambda side: edge_copy(side, k).wait_send())

    def at(turn, lag, task):
        k = turn - lag

        @pl.when(jnp.logical_and(k >= 0, k < chunks))
        def _():
            task(k)

    steps = {
        "Ae": lambda k: multiply(0, k),
        "Be": lambda k: combine(0, k),
        "Re": lambda k: pass_on(0, k),
        "Ce": finish_even,
        "Ct": turned_sum,
        "Rs": one_residual,
        "Dr": drain,
        "Ao": lambda k: multiply(1, k),
        "Bo": lambda k: combine(1, k),
        "Ro": lambda k: pass_on(1, k),
        "Co": finish_odd,
    }

    def run(order):
        def one_turn(turn, carry):
            for name, lag in order:
                at(turn, lag, steps[name])
            return carry

        lax.fori_loop(0, chunks + max(lag for _, lag in order), one_turn, 0)

    @pl.when(first)
    def _():
        run(FIRST_ORDER)

    @pl.when(jnp.logical_and(plain, jnp.logical_not(first)))
    def _():
        run(PLAIN_ORDER)

    @pl.when(later)
    def _():
        run(TURNED_ORDER)

    @pl.when(crossed)
    def _():
        turned_source().wait_send()
        for half in range(2):
            for q in range(nrow):
                whole_part(half, q, out_send.at[half, q]).wait()

    @pl.when(later)
    def _():
        each_pass(lambda half, source: whole_part(half, 0, pass_send.at[half, source]).wait())

    @pl.when(jnp.logical_not(first))
    def _():
        nf_copy().wait_send()


def shards(forcing, inverses, stiffness, pml_layers):
    groups, nrow, ncol = (lax.axis_size(name) for name in ("sweep", "row", "col"))
    _, _, chunks, shot_rows, width = forcing.shape
    chips = ncol // 2
    dma = pltpu.SemaphoreType.DMA
    vmem = pl.BlockSpec(memory_space=pltpu.VMEM)
    return pl.pallas_call(
        functools.partial(sweep_kernel, groups, nrow, ncol),
        name="sweep",
        out_shape=(
            jax.ShapeDtypeStruct(forcing.shape, F32),
            jax.ShapeDtypeStruct((1,) + forcing.shape[1:], F32),
        ),
        in_specs=[
            pl.BlockSpec(memory_space=pl.ANY),
            pl.BlockSpec(memory_space=pl.ANY),
            pl.BlockSpec(memory_space=pl.ANY),
            pl.BlockSpec(memory_space=pltpu.SMEM),
        ],
        out_specs=(vmem, vmem),
        scratch_shapes=[
            pltpu.VMEM(inverses.shape, BF16),
            pltpu.VMEM(forcing.shape, F32),
            pltpu.VMEM((2, chunks, nrow, ROWS, width), BF16),
            pltpu.VMEM((2, chunks, 2, nrow, ROWS, width), BF16),
            pltpu.VMEM((2, chunks, nrow, ROWS, width), BF16),
            pltpu.VMEM((2, chunks, nrow, ROWS, width), BF16),
            pltpu.VMEM((2, chunks, nrow, ROWS, width), BF16),
            pltpu.VMEM((2, chunks, chips, ROWS, width), BF16),
            pltpu.VMEM((chunks, ROWS, width), BF16),
            pltpu.VMEM(forcing.shape[1:], F32),
            pltpu.VMEM((2, chunks, ROWS, 128), BF16),
            pltpu.VMEM((2, chunks, ROWS, 128), BF16),
            pltpu.VMEM(stiffness.shape, F32),
            pltpu.VMEM((chunks, ROWS, width), BF16),
            pltpu.VMEM((chunks, ROWS, width), BF16),
            pltpu.VMEM((2, nrow, width // nrow, 2 * width), BF16),
            pltpu.VMEM((chunks, ROWS, width), BF16),
            pltpu.VMEM((chunks, ROWS, width), BF16),
            dma((2,)),
            dma((3,)),
            dma((5,)),
            dma((2, nrow)),
            dma((2, nrow, SUB)),
            dma((2, nrow)),
            dma((2, nrow)),
            dma((chunks,)),
            dma((chunks,)),
            dma((2, chunks)),
            dma((2, chunks)),
            dma((2, chunks)),
            dma((2, chunks)),
            dma((2, chunks)),
            dma((2, chunks)),
            dma((2, chunks)),
            dma((2, chunks)),
            dma((chunks,)),
            dma((2,)),
            dma((2, chunks)),
            dma((2, chunks)),
        ],
        compiler_params=pltpu.CompilerParams(
            collective_id=0, has_side_effects=True, vmem_limit_bytes=53 * 1024 * 1024
        ),
        cost_estimate=pl.CostEstimate(
            flops=2 * 2 * 8 * 256 * 512 * 1024, bytes_accessed=6 * 2**20, transcendentals=0
        ),
    )(forcing, inverses, stiffness, pml_layers)


def solution(mesh):
    return jax.shard_map(
        shards,
        mesh=mesh,
        in_specs=(
            P("sweep", None, None, "row", "col"),
            P("sweep", None, "col", "row"),
            P("sweep", None),
            P(),
        ),
        out_specs=(P("sweep", None, None, "row", "col"), P("sweep", None, None, "row", "col")),
        check_vma=False,
    )
```

```python
import functools

import jax
import jax.numpy as jnp
from jax import lax
from jax.experimental import pallas as pl
from jax.experimental.pallas import tpu as pltpu
from jax.sharding import PartitionSpec as P

GY = 64
PANEL_PLANES = 8
SIGMA_PEAK = 2.0
MESH = pl.DeviceIdType.MESH
F32 = jnp.float32
BF16 = jnp.bfloat16
FIRST_ORDER = (
    ("Ae", 0), ("Ce", 4), ("Rs", 12), ("Dr", 19), ("Ao", 6), ("Re", 2), ("Co", 10), ("Ro", 8), ("Be", 0), ("Bo", 6),
)
PLAIN_ORDER = (
    ("Dr", 18), ("Ao", 6), ("Co", 9), ("Ce", 4), ("Ae", 0), ("Re", 2), ("Bo", 6), ("Be", 0), ("Rs", 12), ("Ro", 7),
)
TURNED_ORDER = (
    ("Dr", 7), ("Co", 5), ("Ae", 0), ("Ao", 3), ("Rs", 5), ("Be", 0), ("Bo", 3), ("Ce", 3), ("Ct", 1),
)
PLAIN_GROUPS = 2
WAY_STEPS = lambda n: range(n)
WAY_HALVES = (0, 1)
SUB = 2
ROWS = 16


def far_first(count):
    return sorted(range(1, count), key=lambda step: -min(step, count - step))


def sweep_kernel(
    groups, nrow, ncol,
    forcing_hbm, inverses, stiffness, pml, solved, residual,
    weights, sources, loads, parts, sib, total, middle, arrive, onward, next_forcing, edge_out, edge_in,
    stiff_here, turned_out, turned_forcing, held, home_out, home_in,
    w_sem, in_sem, turn_sem, out_send, held_recv, pass_send, part_recv,
    home_send, home_recv, mid_send, mid_recv,
    load_recv, load_send, sib_recv, sib_send, arr_recv, arr_send, fwd_send, nf_sem, edge_send, edge_recv,
):
    chunks = forcing_hbm.shape[2]
    width = forcing_hbm.shape[4]
    forcing = sources
    chips = ncol // 2
    g, r, c = lax.axis_index("sweep"), lax.axis_index("row"), lax.axis_index("col")
    chip, core = c // 2, lax.rem(c, 2)
    sibling = 2 * chip + 1 - core
    first, last = g == 0, g == groups - 1
    left_end, right_end = c == 0, c == ncol - 1
    plain = g < PLAIN_GROUPS
    later = jnp.logical_not(plain)
    diagonal = r == chip
    partner = (g, chip, 2 * r + core)
    crossed = jnp.logical_and(later, jnp.logical_not(diagonal))

    def column(other_row):
        return (g, other_row, c)

    def along(other_chip):
        return (g, r, 2 * other_chip + core)

    w_copies = [
        pltpu.make_async_copy(inverses.at[p], weights.at[p], w_sem.at[p]) for p in range(2)
    ]
    begin = pl.multiple_of(c * width, 128)
    in_copies = [
        pltpu.make_async_copy(forcing_hbm.at[0], sources.at[0], in_sem.at[0]),
        pltpu.make_async_copy(forcing_hbm.at[1], sources.at[1], in_sem.at[1]),
        pltpu.make_async_copy(stiffness, stiff_here, in_sem.at[2]),
    ]
    for copy in in_copies + w_copies[:1]:
        copy.start()

    @pl.when(jnp.logical_not(crossed))
    def _():
        w_copies[1].start()

    barrier = pltpu.get_barrier_semaphore()

    def greet(device):
        pl.semaphore_signal(barrier, inc=1, device_id=device, device_id_type=MESH)

    for step in far_first(nrow):
        greet(column(lax.rem(r + step, nrow)))
    greet((g, r, sibling))
    for step in far_first(chips):
        greet(along(lax.rem(chip + step, chips)))
    for other in range(nrow):
        @pl.when(jnp.logical_not(last))
        def _():
            greet((g + 1, other, c))

        @pl.when(jnp.logical_not(first))
        def _():
            greet((g - 1, other, c))

    @pl.when(crossed)
    def _():
        for step in far_first(chips):
            greet((g, chip, 2 * lax.rem(chip + step, chips) + core))
        for step in far_first(nrow):
            greet((g, lax.rem(r + step, nrow), 2 * r + core))

    @pl.when(jnp.logical_not(left_end))
    def _():
        greet((g, r, c - 1))

    @pl.when(jnp.logical_not(right_end))
    def _():
        greet((g, r, c + 1))

    @pl.when(first)
    def _():
        in_copies[0].wait()
        for k in range(chunks):
            loads[0, k, r] = forcing[0, :, k].reshape(ROWS, width).astype(BF16)

    @pl.when(left_end)
    def _():
        edge_in[0] = jnp.zeros_like(edge_in[0])

    @pl.when(right_end)
    def _():
        edge_in[1] = jnp.zeros_like(edge_in[1])

    expected = (nrow - 1) + 1 + (chips - 1)
    expected = expected + nrow * (2 - first.astype(jnp.int32) - last.astype(jnp.int32))
    expected = expected + (nrow + chips - 2) * crossed.astype(jnp.int32)
    expected = expected + 2 - left_end.astype(jnp.int32) - right_end.astype(jnp.int32)
    pl.semaphore_wait(barrier, expected)

    def load_copy(p, k, step):
        return pltpu.make_async_remote_copy(
            src_ref=loads.at[p, k, r], dst_ref=loads.at[p, k, r],
            send_sem=load_send.at[p, k], recv_sem=load_recv.at[p, k],
            device_id=column(lax.rem(r + step, nrow)), device_id_type=MESH,
        )

    def forward_copy(k, other):
        return pltpu.make_async_remote_copy(
            src_ref=onward.at[k], dst_ref=loads.at[0, k, r],
            send_sem=fwd_send.at[k], recv_sem=load_recv.at[0, k],
            device_id=(g + 1, other, c), device_id_type=MESH,
        )

    def sib_copy(p, k):
        return pltpu.make_async_remote_copy(
            src_ref=parts.at[p, k, 1 - core], dst_ref=sib.at[p, k],
            send_sem=sib_send.at[p, k], recv_sem=sib_recv.at[p, k],
            device_id=(g, r, sibling), device_id_type=MESH,
        )

    def middle_copy(p, k, step):
        other = lax.rem(r + step, nrow)
        return pltpu.make_async_remote_copy(
            src_ref=total.at[p, k, other], dst_ref=middle.at[p, k, r],
            send_sem=mid_send.at[p, k], recv_sem=mid_recv.at[p, k],
            device_id=column(other), device_id_type=MESH,
        )

    def row_copy(p, k, step):
        other = lax.rem(chip + step, chips)
        return pltpu.make_async_remote_copy(
            src_ref=total.at[p, k, other], dst_ref=arrive.at[p, k, chip],
            send_sem=arr_send.at[p, k], recv_sem=arr_recv.at[p, k],
            device_id=along(other), device_id_type=MESH,
        )

    def home_copy(p, k, step):
        other = lax.rem(chip + step, chips)
        return pltpu.make_async_remote_copy(
            src_ref=middle.at[p, k, other], dst_ref=arrive.at[p, k, chip],
            send_sem=arr_send.at[p, k], recv_sem=arr_recv.at[p, k],
            device_id=along(other), device_id_type=MESH,
        )

    def row_load_copy(k, step):
        return pltpu.make_async_remote_copy(
            src_ref=loads.at[1, k, chip], dst_ref=loads.at[1, k, chip],
            send_sem=load_send.at[1, k], recv_sem=load_recv.at[1, k],
            device_id=along(lax.rem(chip + step, chips)), device_id_type=MESH,
        )

    def solved_copy(k):
        return pltpu.make_async_remote_copy(
            src_ref=home_out.at[k], dst_ref=home_in.at[k],
            send_sem=home_send.at[k], recv_sem=home_recv.at[k],
            device_id=partner, device_id_type=MESH,
        )

    part_rows = width // nrow

    sub_rows = part_rows // SUB

    def part(index, sub=None):
        start = index * part_rows
        if sub is None:
            return pl.ds(pl.multiple_of(start, part_rows), part_rows)
        return pl.ds(pl.multiple_of(start + sub * sub_rows, sub_rows), sub_rows)

    def turned_source():
        return pltpu.make_async_remote_copy(
            src_ref=turned_out, dst_ref=turned_forcing,
            send_sem=turn_sem.at[1], recv_sem=turn_sem.at[2],
            device_id=partner, device_id_type=MESH,
        )

    def out_copy(half, q, sub, direct):
        rows = part(q, sub)
        if direct:
            landing, landed_sem = weights.at[1, half, rows], part_recv.at[half, q]
        else:
            landing, landed_sem = held.at[half, r, part(0, sub)], held_recv.at[half, r, sub]
        return pltpu.make_async_remote_copy(
            src_ref=inverses.at[1, half, rows], dst_ref=landing,
            send_sem=out_send.at[half, q], recv_sem=landed_sem,
            device_id=(g, chip, 2 * q + core) if half == 0 or direct else (g, q, c),
            device_id_type=MESH,
        )

    def held_part(half, source, sub):
        here = held.at[half, source, part(0, sub)]
        return pltpu.make_async_copy(here, here, held_recv.at[half, source, sub])

    def pass_copy(half, source, sub):
        index = chip if half == 0 else r
        return pltpu.make_async_remote_copy(
            src_ref=held.at[half, source, part(0, sub)],
            dst_ref=weights.at[1, half, part(index, sub)],
            send_sem=pass_send.at[half, source], recv_sem=part_recv.at[half, index],
            device_id=(g, r if half == 0 else chip, 2 * source + core), device_id_type=MESH,
        )

    def whole_part(half, q, sem):
        here = weights.at[1, half, part(q)]
        return pltpu.make_async_copy(here, here, sem)

    ways = [(half, step) for step in WAY_STEPS(nrow) for half in WAY_HALVES]

    def start_out():
        for sub in range(SUB):
            for half, step in ways:
                q = lax.rem((chip if half == 0 else r) + step, nrow)

                @pl.when(r == q)
                def _():
                    out_copy(half, q, sub, True).start()

                @pl.when(r != q)
                def _():
                    out_copy(half, q, sub, False).start()

    def each_pass(act):
        for half, step in ways:
            source = lax.rem(r + step, nrow)

            @pl.when(jnp.logical_and(source != r, source != chip))
            def _():
                act(half, source)

    def nf_copy():
        return pltpu.make_async_remote_copy(
            src_ref=forcing_hbm.at[0], dst_ref=next_forcing,
            send_sem=nf_sem.at[0], recv_sem=nf_sem.at[1],
            device_id=(g - 1, r, c), device_id_type=MESH,
        )

    def edge_copy(side, k):
        return pltpu.make_async_remote_copy(
            src_ref=edge_out.at[side, k], dst_ref=edge_in.at[1 - side, k],
            send_sem=edge_send.at[side, k], recv_sem=edge_recv.at[1 - side, k],
            device_id=(g, r, c - 1 + 2 * side), device_id_type=MESH,
        )

    def each_edge(act):
        for side, end in ((0, left_end), (1, right_end)):
            @pl.when(jnp.logical_not(end))
            def _():
                act(side)

    def landed(buffer, count, sem):
        some = buffer.at[pl.ds(0, count)]
        pltpu.make_async_copy(some, some, sem).wait()

    def wait_loads(p, k):
        if p == 1:
            landed(loads.at[p, k], nrow - 1, load_recv.at[p, k])

            @pl.when(jnp.logical_and(jnp.logical_not(crossed), k == 0))
            def _():
                w_copies[1].wait()

            @pl.when(jnp.logical_and(crossed, k == 0))
            def _():
                for half in range(2):
                    for q in range(nrow):
                        whole_part(half, q, part_recv.at[half, q]).wait()
        else:
            @pl.when(first)
            def _():
                landed(loads.at[p, k], nrow - 1, load_recv.at[p, k])

            @pl.when(jnp.logical_not(first))
            def _():
                landed(loads.at[p, k], nrow, load_recv.at[p, k])

    def multiply(p, k):
        wait_loads(p, k)
        rows = nrow * ROWS
        left = loads[p, k].reshape(rows, width)
        by_real = jnp.dot(left, weights[p, 0], preferred_element_type=F32)
        by_imag = jnp.dot(left, weights[p, 1], preferred_element_type=F32)
        by_real = by_real.reshape(nrow, 2, 8, 2 * width)
        by_imag = by_imag.reshape(nrow, 2, 8, 2 * width)
        real = by_real[:, 0] - by_imag[:, 1]
        imag = by_real[:, 1] + by_imag[:, 0]
        both = jnp.concatenate([real[:, None], imag[:, None]], axis=1).reshape(nrow, ROWS, 2 * width)
        both = both.astype(BF16)
        parts[p, k, 0] = both[:, :, :width]
        parts[p, k, 1] = both[:, :, width:]
        sib_copy(p, k).start()

    def combine(p, k):
        sib_copy(p, k).wait_recv()
        whole = parts[p, k, core].astype(F32) + sib[p, k].astype(F32)

        total[p, k] = whole.astype(BF16)

        def to_rows():
            middle[p, k, r] = total[p, k, r]
            for step in far_first(nrow):
                middle_copy(p, k, step).start()

        if p == 1:
            to_rows()
        else:
            pl.when(plain)(to_rows)

            @pl.when(later)
            def _():
                arrive[p, k, chip] = total[p, k, chip]
                for step in far_first(chips):
                    row_copy(p, k, step).start()

    def row_sum(p, k):
        landed(arrive.at[p, k], chips - 1, arr_recv.at[p, k])
        return jnp.sum(arrive[p, k].astype(F32), axis=0)

    def middle_landed(p, k):
        landed(middle.at[p, k], nrow - 1, mid_recv.at[p, k])

    def pass_on(p, k):
        middle_landed(p, k)
        for step in far_first(chips):
            home_copy(p, k, step).start()
        arrive[p, k, chip] = middle[p, k, chip]

    def keep(p, k, value):
        solved[p, 0, k] = value[:8]
        solved[p, 1, k] = value[8:]
        if p == 0:
            edge_out[0, k] = value[:, :128].astype(BF16)
            edge_out[1, k] = value[:, width - 128 :].astype(BF16)
            each_edge(lambda side: edge_copy(side, k).start())

    def forward(k, value):
        @pl.when(jnp.logical_and(jnp.logical_not(last), k == 0))
        def _():
            nf_copy().wait_recv()

        @pl.when(jnp.logical_not(last))
        def _():
            source = next_forcing[:, k].reshape(ROWS, width)
            onward[k] = (value + source).astype(BF16)
            for step in far_first(nrow) + [0]:
                forward_copy(k, lax.rem(r + step, nrow)).start()

        keep(1, k, value)

    def turned_sum(k):
        own = row_sum(0, k)
        loads[1, k, chip] = (own + turned_forcing[k].astype(F32)).astype(BF16)
        for step in far_first(chips):
            row_load_copy(k, step).start()

        @pl.when(diagonal)
        def _():
            keep(0, k, own)

        @pl.when(crossed)
        def _():
            home_out[k] = own.astype(BF16)
            solved_copy(k).start()

    def finish_even(k):
        @pl.when(plain)
        def _():
            value = row_sum(0, k)
            source = forcing[1, :, k].reshape(ROWS, width)
            loads[1, k, r] = (value + source).astype(BF16)
            for step in far_first(nrow):
                load_copy(1, k, step).start()
            keep(0, k, value)

        @pl.when(crossed)
        def _():
            solved_copy(k).wait_recv()
            keep(0, k, home_in[k].astype(F32))

    def finish_odd(k):
        @pl.when(plain)
        def _():
            forward(k, row_sum(1, k))

        @pl.when(later)
        def _():
            middle_landed(1, k)
            forward(k, jnp.sum(middle[1, k].astype(F32), axis=0))

    @pl.when(first)
    def _():
        for k in range(chunks):
            for step in far_first(nrow):
                load_copy(0, k, step).start()

    @pl.when(jnp.logical_not(first))
    def _():
        nf_copy().start()

    pl.when(crossed)(start_out)

    @pl.when(later)
    def _():
        in_copies[1].wait()
        for k in range(chunks):
            turned_out[k] = forcing[1, :, k].reshape(ROWS, width).astype(BF16)

        @pl.when(diagonal)
        def _():
            turned_forcing[...] = turned_out[...]

        @pl.when(crossed)
        def _():
            turned_source().start()

    w_copies[0].wait()

    @pl.when(later)
    def _():
        for sub in range(SUB):
            def pass_part(half, source):
                held_part(half, source, sub).wait()
                pass_copy(half, source, sub).start()

            each_pass(pass_part)

    @pl.when(crossed)
    def _():
        turned_source().wait_recv()

    @pl.when(plain)
    def _():
        in_copies[1].wait()

    @pl.when(jnp.logical_not(first))
    def _():
        in_copies[0].wait()

    in_copies[2].wait()

    def spread(number):
        return jnp.full((8, width), number, jnp.int32).astype(F32)

    top, bottom = spread(pml[0]), spread(pml[1])
    centre_plane = spread(2 * g).astype(F32) * PANEL_PLANES + PANEL_PLANES / 2.0
    from_end = 2 * groups * PANEL_PLANES - centre_plane
    upper = jnp.maximum(top - centre_plane, 0.0) / top
    lower = jnp.maximum(bottom - from_end, 0.0) / bottom
    sigma = SIGMA_PEAK * (upper * upper + lower * lower)
    stiff = jnp.broadcast_to(stiff_here[0:1, pl.ds(begin, width)], (8, width))
    centre = 6.0 - stiff
    absorb = stiff * sigma
    line = lax.rem(lax.broadcasted_iota(jnp.int32, (ROWS, width), 1), GY)
    not_low, not_high = line > 0, line < GY - 1

    def one_residual(k):
        each_edge(lambda side: edge_copy(1 - side, k).wait_recv())
        real, imag = solved[0, 0, k], solved[0, 1, k]
        wave = jnp.concatenate([real, imag], axis=0)
        padded = jnp.concatenate(
            [edge_in[0, k].astype(F32), wave, edge_in[1, k].astype(F32)], axis=1
        )
        span = width + 256

        def moved(distance):
            turned = pltpu.roll(padded, distance % span, 1)
            return turned[:, 128 : 128 + width]

        beside = moved(GY) + moved(-GY)
        beside = beside + jnp.where(not_low, moved(1), 0.0) + jnp.where(not_high, moved(-1), 0.0)
        load = loads[0, k, r].astype(F32)
        real_applied = centre * real + absorb * imag - beside[:8]
        imag_applied = centre * imag - absorb * real - beside[8:]
        residual[0, 0, k] = load[:8] - real_applied + solved[1, 0, k]
        residual[0, 1, k] = load[8:] - imag_applied + solved[1, 1, k]

    def drain(k):
        for p in range(2):
            sib_copy(p, k).wait_send()
        landed(total.at[1, k], nrow - 1, mid_send.at[1, k])
        landed(loads.at[1, k], nrow - 1, load_send.at[1, k])
        landed(total.at[0, k], chips - 1, arr_send.at[0, k])

        @pl.when(plain)
        def _():
            landed(total.at[0, k], nrow - 1, mid_send.at[0, k])
            landed(middle.at[1, k], chips - 1, arr_send.at[1, k])

        @pl.when(first)
        def _():
            landed(loads.at[0, k], nrow - 1, load_send.at[0, k])

        @pl.when(crossed)
        def _():
            solved_copy(k).wait_send()

        @pl.when(jnp.logical_not(last))
        def _():
            landed(loads.at[0, k], nrow, fwd_send.at[k])

        each_edge(lambda side: edge_copy(side, k).wait_send())

    def at(turn, lag, task):
        k = turn - lag

        @pl.when(jnp.logical_and(k >= 0, k < chunks))
        def _():
            task(k)

    steps = {
        "Ae": lambda k: multiply(0, k),
        "Be": lambda k: combine(0, k),
        "Re": lambda k: pass_on(0, k),
        "Ce": finish_even,
        "Ct": turned_sum,
        "Rs": one_residual,
        "Dr": drain,
        "Ao": lambda k: multiply(1, k),
        "Bo": lambda k: combine(1, k),
        "Ro": lambda k: pass_on(1, k),
        "Co": finish_odd,
    }

    def run(order):
        def one_turn(turn, carry):
            for name, lag in order:
                at(turn, lag, steps[name])
            return carry

        lax.fori_loop(0, chunks + max(lag for _, lag in order), one_turn, 0)

    @pl.when(first)
    def _():
        run(FIRST_ORDER)

    @pl.when(jnp.logical_and(plain, jnp.logical_not(first)))
    def _():
        run(PLAIN_ORDER)

    @pl.when(later)
    def _():
        run(TURNED_ORDER)

    @pl.when(crossed)
    def _():
        turned_source().wait_send()
        for half in range(2):
            for q in range(nrow):
                whole_part(half, q, out_send.at[half, q]).wait()

    @pl.when(later)
    def _():
        each_pass(lambda half, source: whole_part(half, 0, pass_send.at[half, source]).wait())

    @pl.when(jnp.logical_not(first))
    def _():
        nf_copy().wait_send()


def shards(forcing, inverses, stiffness, pml_layers):
    groups, nrow, ncol = (lax.axis_size(name) for name in ("sweep", "row", "col"))
    _, _, chunks, shot_rows, width = forcing.shape
    chips = ncol // 2
    dma = pltpu.SemaphoreType.DMA
    vmem = pl.BlockSpec(memory_space=pltpu.VMEM)
    return pl.pallas_call(
        functools.partial(sweep_kernel, groups, nrow, ncol),
        name="sweep",
        out_shape=(
            jax.ShapeDtypeStruct(forcing.shape, F32),
            jax.ShapeDtypeStruct((1,) + forcing.shape[1:], F32),
        ),
        in_specs=[
            pl.BlockSpec(memory_space=pl.ANY),
            pl.BlockSpec(memory_space=pl.ANY),
            pl.BlockSpec(memory_space=pl.ANY),
            pl.BlockSpec(memory_space=pltpu.SMEM),
        ],
        out_specs=(vmem, vmem),
        scratch_shapes=[
            pltpu.VMEM(inverses.shape, BF16),
            pltpu.VMEM(forcing.shape, F32),
            pltpu.VMEM((2, chunks, nrow, ROWS, width), BF16),
            pltpu.VMEM((2, chunks, 2, nrow, ROWS, width), BF16),
            pltpu.VMEM((2, chunks, nrow, ROWS, width), BF16),
            pltpu.VMEM((2, chunks, nrow, ROWS, width), BF16),
            pltpu.VMEM((2, chunks, nrow, ROWS, width), BF16),
            pltpu.VMEM((2, chunks, chips, ROWS, width), BF16),
            pltpu.VMEM((chunks, ROWS, width), BF16),
            pltpu.VMEM(forcing.shape[1:], F32),
            pltpu.VMEM((2, chunks, ROWS, 128), BF16),
            pltpu.VMEM((2, chunks, ROWS, 128), BF16),
            pltpu.VMEM(stiffness.shape, F32),
            pltpu.VMEM((chunks, ROWS, width), BF16),
            pltpu.VMEM((chunks, ROWS, width), BF16),
            pltpu.VMEM((2, nrow, width // nrow, 2 * width), BF16),
            pltpu.VMEM((chunks, ROWS, width), BF16),
            pltpu.VMEM((chunks, ROWS, width), BF16),
            dma((2,)),
            dma((3,)),
            dma((5,)),
            dma((2, nrow)),
            dma((2, nrow, SUB)),
            dma((2, nrow)),
            dma((2, nrow)),
            dma((chunks,)),
            dma((chunks,)),
            dma((2, chunks)),
            dma((2, chunks)),
            dma((2, chunks)),
            dma((2, chunks)),
            dma((2, chunks)),
            dma((2, chunks)),
            dma((2, chunks)),
            dma((2, chunks)),
            dma((chunks,)),
            dma((2,)),
            dma((2, chunks)),
            dma((2, chunks)),
        ],
        compiler_params=pltpu.CompilerParams(
            collective_id=0, has_side_effects=True, vmem_limit_bytes=53 * 1024 * 1024
        ),
        cost_estimate=pl.CostEstimate(
            flops=2 * 2 * 8 * 256 * 512 * 1024, bytes_accessed=6 * 2**20, transcendentals=0
        ),
    )(forcing, inverses, stiffness, pml_layers)


def solution(mesh):
    return jax.shard_map(
        shards,
        mesh=mesh,
        in_specs=(
            P("sweep", None, None, "row", "col"),
            P("sweep", None, "col", "row"),
            P("sweep", None),
            P(),
        ),
        out_specs=(P("sweep", None, None, "row", "col"), P("sweep", None, None, "row", "col")),
        check_vma=False,
    )
```
